512 devices in a mesh: section: 8 (over z), node: 8 (over x, core), local: 8 (over y).
Axes of the slice: x: 4, y: 8, z: 8, core: 2. Of those that a mesh axis runs over, the one named last changes fastest.
Arguments:
- section_inputs: bfloat16 [8, 64, 4, 196, 512], P('section', ('node', 'local')), may hold values from -6 to 6
- grad_in: bfloat16 [8, 64, 196, 512], P('section', ('node', 'local')), may hold values from -6 to 6
- loss_grad: bfloat16 [64, 3, 196, 512], P(('node', 'local')), may hold values from -6 to 6
- w_reduce: bfloat16 [8, 512, 256], P('section'), may hold values from -0.25 to 0.25
- w_spatial: bfloat16 [8, 2304, 256], P('section'), may hold values from -0.125 to 0.125
- w_expand: bfloat16 [8, 256, 512], P('section'), may hold values from -0.375 to 0.375
- err_reduce: bfloat16 [8, 64, 512, 256], P('section', ('node', 'local')), may hold values from -360 to 360
- err_spatial: bfloat16 [8, 64, 2304, 256], P('section', ('node', 'local')), may hold values from -360 to 360
- err_expand: bfloat16 [8, 64, 256, 512], P('section', ('node', 'local')), may hold values from -360 to 360
- prior_reduce: float32 [8, 32, 256], P('section'), may hold values from -6 to 6
- prior_spatial: float32 [8, 32, 256], P('section'), may hold values from -6 to 6
- prior_expand: float32 [8, 32, 512], P('section'), may hold values from -6 to 6
Outputs:
- leaving: bfloat16 [8, 64, 196, 512], P('section', ('node', 'local'))
- basis_reduce: float32 [8, 32, 512], P('section', None, ('node', 'local'))
- basis_spatial: float32 [8, 32, 2304], P('section', None, ('node', 'local'))
- basis_expand: float32 [8, 32, 256], P('section', None, ('node', 'local'))
- right_reduce: float32 [8, 32, 256], P('section', None, ('node', 'local'))
- right_spatial: float32 [8, 32, 256], P('section', None, ('node', 'local'))
- right_expand: float32 [8, 32, 512], P('section', None, ('node', 'local'))
The draws below stay inside these ranges and needn't reach their ends.
All inputs are finite; a program needn't handle non-finite values.
Results may differ from the reference program's by a relative error of at most 0.0095.
Values may be sent and summed in bfloat16 or wider, within the bound.
A program may use at most 128 MiB of HBM per device.

```python
import functools
import math
import jax
import jax.numpy as jnp
from jax import lax

OUT = 512
MID = 256
SIDE = 14
RANK = 32
TICKS = 4
SECTIONS = 8
REPL = 64


def scaled_error(key, salt, row_count, col_count):
    subkeys = jax.random.split(jax.random.fold_in(key, salt), 4)
    full_shape = (SECTIONS, REPL, row_count, col_count)
    rising = 1.0 + 2.0 * jnp.arange(row_count, dtype=jnp.float32) / max(row_count - 1, 1)
    row_scale = jnp.exp(jax.random.uniform(subkeys[0], (SECTIONS, REPL, row_count, 1), jnp.float32) * math.log(10.0))
    random_part = jnp.clip(jax.random.normal(subkeys[3], full_shape, jnp.float32), -4.0, 4.0)
    col_scale = jnp.exp(jax.random.uniform(subkeys[1], (SECTIONS, REPL, 1, col_count), jnp.float32) * math.log(10.0))
    return 0.3 * random_part * row_scale * rising[:, None] * col_scale


def draw_err_reduce(key, part):
    return scaled_error(key, 11, OUT, MID).astype(jnp.bfloat16)


def draw_err_spatial(key, part):
    return scaled_error(key, 12, 9 * MID, MID).astype(jnp.bfloat16)


def draw_err_expand(key, part):
    return scaled_error(key, 13, MID, OUT).astype(jnp.bfloat16)


def shard_levels(stream_key, dims, cuts, low, top_value):
    def one(axis_at, blocks):
        draws = jax.random.uniform(jax.random.fold_in(jax.random.fold_in(stream_key, 6), axis_at), (blocks,), jnp.float32, low / len(cuts), top_value / len(cuts))
        return jnp.repeat(jnp.exp(draws), dims[axis_at] // blocks).reshape((-1,) + (1,) * (len(dims) - axis_at - 1))

    factor_of = one(*cuts[0])
    for cut in cuts[1:]:
        factor_of = factor_of * one(*cut)
    return factor_of


def centred(stream_key, dims, deviation, bound, shards=(), kind=jnp.bfloat16):
    loudness = shard_levels(stream_key, dims, shards, -0.22, 0.18) if shards else 1.0
    values = jax.random.normal(stream_key, dims, jnp.float32) * deviation * loudness
    return jnp.minimum(jnp.maximum(values, -bound), bound).astype(kind)


def setup_inputs(seed: int = 0) -> dict:
    key_of = jax.random.split(jax.random.key(seed), 13)
    section_inputs = centred(key_of[0], (SECTIONS, REPL, TICKS, SIDE * SIDE, OUT), 1.0, 6.0, ((0, 8), (1, 64)))
    grad_in = centred(key_of[1], (SECTIONS, REPL, SIDE * SIDE, OUT), 1.0, 6.0, ((0, 8), (1, 64)))
    loss_grad = centred(key_of[2], (REPL, TICKS - 1, SIDE * SIDE, OUT), 1.0, 6.0, ((0, 64),))
    w_reduce = centred(key_of[3], (SECTIONS, OUT, MID), OUT ** -0.5, 0.25, ((0, 8),))
    w_spatial = centred(key_of[4], (SECTIONS, 9 * MID, MID), (9 * MID) ** -0.5, 0.125, ((0, 8),))
    w_expand = centred(key_of[5], (SECTIONS, MID, OUT), MID ** -0.5, 0.375, ((0, 8),))
    err_reduce = draw_err_reduce(jax.random.fold_in(key_of[12], 71), 0)
    err_spatial = draw_err_spatial(jax.random.fold_in(key_of[12], 71), 0)
    err_expand = draw_err_expand(jax.random.fold_in(key_of[12], 71), 0)
    prior_reduce = centred(key_of[9], (SECTIONS, RANK, MID), 1.0, 6.0, ((0, 8),), jnp.float32)
    prior_spatial = centred(key_of[10], (SECTIONS, RANK, MID), 1.0, 6.0, ((0, 8),), jnp.float32)
    prior_expand = centred(key_of[11], (SECTIONS, RANK, OUT), 1.0, 6.0, ((0, 8),), jnp.float32)
    return dict(section_inputs=section_inputs, grad_in=grad_in, loss_grad=loss_grad, w_reduce=w_reduce, w_spatial=w_spatial, w_expand=w_expand, err_reduce=err_reduce, err_spatial=err_spatial, err_expand=err_expand, prior_reduce=prior_reduce, prior_spatial=prior_spatial, prior_expand=prior_expand)


precise = lax.Precision.HIGHEST

def silu_slope(values):
    logistic = jax.nn.sigmoid(values)
    return logistic * (1.0 + values * (1.0 - logistic))

def expand_taps(hidden, image_side):
    channels = hidden.shape[-1]
    padded = jnp.pad(hidden.reshape(image_side, image_side, channels), ((1, 1), (1, 1), (0, 0)))
    pieces = [padded[row_off:row_off + image_side, col_off:col_off + image_side, :] for row_off in range(3) for col_off in range(3)]
    return jnp.concatenate(pieces, axis=-1).reshape(image_side * image_side, 9 * channels)

def fold_taps(columns, image_side):
    channels = columns.shape[-1] // 9
    blocks = columns.reshape(image_side, image_side, 9, channels)
    running = jnp.zeros((image_side + 2, image_side + 2, channels), jnp.float32)
    for row_off in range(3):
        for col_off in range(3):
            placed = jnp.pad(blocks[:, :, 3 * row_off + col_off, :], ((row_off, 2 - row_off), (col_off, 2 - col_off), (0, 0)))
            running = running + placed
    return running[1:image_side + 1, 1:image_side + 1, :].reshape(image_side * image_side, channels)

def block_backward(inputs, upstream, reduce_weight, spatial_weight, expand_weight, image_side):
    pre_reduce = jnp.dot(inputs.astype(jnp.float32), reduce_weight.astype(jnp.float32), preferred_element_type=jnp.float32)
    hidden_one = jax.nn.silu(pre_reduce).astype(jnp.bfloat16)
    columns = expand_taps(hidden_one, image_side)
    pre_spatial = jnp.dot(columns.astype(jnp.float32), spatial_weight.astype(jnp.float32), preferred_element_type=jnp.float32)
    hidden_two = jax.nn.silu(pre_spatial).astype(jnp.bfloat16)
    back_two = jnp.dot(upstream.astype(jnp.float32), expand_weight.T.astype(jnp.float32), preferred_element_type=jnp.float32)
    back_spatial = (back_two * silu_slope(pre_spatial)).astype(jnp.bfloat16)
    back_columns = jnp.dot(back_spatial.astype(jnp.float32), spatial_weight.T.astype(jnp.float32), preferred_element_type=jnp.float32)
    back_one = fold_taps(back_columns, image_side)
    back_reduce = (back_one * silu_slope(pre_reduce)).astype(jnp.bfloat16)
    leaving = (upstream.astype(jnp.float32) + jnp.dot(back_reduce.astype(jnp.float32), reduce_weight.T.astype(jnp.float32), preferred_element_type=jnp.float32)).astype(jnp.bfloat16)
    gradients = (jnp.dot(inputs.T.astype(jnp.float32), back_reduce.astype(jnp.float32), preferred_element_type=jnp.float32), jnp.dot(columns.T.astype(jnp.float32), back_spatial.astype(jnp.float32), preferred_element_type=jnp.float32), jnp.dot(hidden_two.T.astype(jnp.float32), upstream.astype(jnp.float32), preferred_element_type=jnp.float32))
    return (leaving, gradients)

def compress(gradients, errors, prior):
    matrices = gradients + errors.astype(jnp.float32)
    row_count = matrices.shape[1]
    factor = jnp.einsum('kc,rnc->kn', prior, matrices, precision=precise)
    gram_value = jnp.dot(factor, factor.T, precision=precise)
    triangle = jnp.linalg.cholesky(gram_value)
    orthonormal = lax.linalg.triangular_solve(triangle, factor, left_side=True, lower=True)
    scaled_basis = math.sqrt(row_count) * orthonormal
    loading = jnp.einsum('kn,rnc->kc', orthonormal, matrices, precision=precise) / (REPL * math.sqrt(row_count))
    return (scaled_basis, loading)

def reference(section_inputs, grad_in, loss_grad, w_reduce, w_spatial, w_expand, err_reduce, err_spatial, err_expand, prior_reduce, prior_spatial, prior_expand):
    run_block = jax.vmap(functools.partial(block_backward, image_side=SIDE), in_axes=(0, 0, None, None, None))
    last_flags = jnp.arange(SECTIONS) == SECTIONS - 1

    def one_section(carry_next, section_slice):
        inputs, first_grad, reduce_weight, spatial_weight, expand_weight, error_reduce, error_spatial, error_expand, old_reduce, old_spatial, old_expand, last_section = section_slice
        upstream = first_grad
        totals = (jnp.zeros((REPL, OUT, MID), jnp.float32), jnp.zeros((REPL, 9 * MID, MID), jnp.float32), jnp.zeros((REPL, MID, OUT), jnp.float32))
        handed = []
        for tick_index in range(TICKS):
            if tick_index > 0:
                upstream = jnp.where(last_section, loss_grad[:, tick_index - 1], carry_next[:, tick_index - 1])
            leaving, gradients = run_block(inputs[:, tick_index], upstream, reduce_weight, spatial_weight, expand_weight)
            handed.append(leaving)
            totals = tuple((totals[member] + gradients[member] for member in range(3)))
        basis_one, loading_one = compress(totals[0], error_reduce, old_reduce)
        basis_two, loading_two = compress(totals[1], error_spatial, old_spatial)
        basis_three, loading_three = compress(totals[2], error_expand, old_expand)
        return (jnp.stack(handed, axis=1), (handed[-1], basis_one, basis_two, basis_three, loading_one, loading_two, loading_three))
    initial = jnp.zeros((REPL, TICKS, SIDE * SIDE, OUT), jnp.bfloat16)
    section_data = (section_inputs, grad_in, w_reduce, w_spatial, w_expand, err_reduce, err_spatial, err_expand, prior_reduce, prior_spatial, prior_expand, last_flags)
    final_carry, stacked = lax.scan(one_section, initial, section_data, reverse=True)
    return (stacked[0], stacked[1], stacked[2], stacked[3], stacked[4], stacked[5], stacked[6])
```

```python
import functools
import math

import jax
import jax.numpy as jnp
from jax import lax
from jax.experimental import pallas as pl
from jax.experimental.pallas import tpu as pltpu
from jax.sharding import PartitionSpec as P

SIDE = 14
PITCH = 16
ROWS = SIDE * PITCH
BLOCK = 256
PIXELS = SIDE * SIDE
TICKS = 4
OUT = 512
MID = 256
RANK = 32
TAPS = 9 * MID
COLUMNS = OUT + TAPS + MID
LANES = 128
TILED = COLUMNS // LANES * RANK
MESH = pl.DeviceIdType.MESH
F32 = jnp.float32
BF16 = jnp.bfloat16
PARTS = ((0, OUT), (OUT, TAPS), (OUT + TAPS, MID))


def dot(a, b):
    return jnp.dot(a, b, preferred_element_type=F32)


def dot_t(a, b):
    return lax.dot_general(a, b, (((1,), (1,)), ((), ())), preferred_element_type=F32)


def precise_dot_t(a, b):
    return lax.dot_general(
        a, b, (((1,), (1,)), ((), ())), preferred_element_type=F32, precision=lax.Precision.HIGHEST
    )


def precise_dot(a, b):
    return jnp.dot(a, b, preferred_element_type=F32, precision=lax.Precision.HIGHEST)


def two_terms(values):
    high = values.astype(BF16)
    low = (values - high.astype(F32)).astype(BF16)
    return jnp.concatenate([high, low], axis=0)


def folded(values):
    return values[:RANK] + values[RANK:]


def sigmoid(values):
    return 1.0 / (1.0 + jnp.exp(-values))


def spread_matrix():
    row = lax.broadcasted_iota(jnp.int32, (ROWS, PIXELS), 0)
    pixel = lax.broadcasted_iota(jnp.int32, (ROWS, PIXELS), 1)
    hit = ((row // PITCH) * SIDE + row % PITCH == pixel) & (row % PITCH < SIDE)
    return jnp.where(hit, 1.0, 0.0).astype(BF16)


def gather_matrix():
    row = lax.broadcasted_iota(jnp.int32, (PIXELS, ROWS), 1)
    pixel = lax.broadcasted_iota(jnp.int32, (PIXELS, ROWS), 0)
    hit = ((row // PITCH) * SIDE + row % PITCH == pixel) & (row % PITCH < SIDE)
    return jnp.where(hit, 1.0, 0.0).astype(BF16)


def shifted_copies(values, ref):
    ref[1, PITCH : PITCH + ROWS, :] = values.astype(BF16)
    ref[0, PITCH : PITCH + ROWS, :] = pltpu.roll(values, 1, 0).astype(BF16)
    ref[2, PITCH : PITCH + ROWS, :] = pltpu.roll(values, ROWS - 1, 0).astype(BF16)


def kernel(
    sizes,
    x_ref,
    grad_ref,
    loss_ref,
    wr_ref,
    ws_ref,
    we_ref,
    er_ref,
    es_ref,
    ee_ref,
    pr_ref,
    ps_ref,
    pe_ref,
    leaving_ref,
    basis_r_ref,
    basis_s_ref,
    basis_e_ref,
    right_r_ref,
    right_s_ref,
    right_e_ref,
    spread,
    x_all,
    cols,
    h2_all,
    ga_all,
    gb_all,
    up_all,
    shift,
    gshift,
    slope1,
    slope2,
    prior_rs,
    prior_e,
    acc,
    sent,
    arrived,
    tiled,
    core_in,
    half,
    y_in,
    x_in,
    full,
    pt2,
    right_tiles,
    right_tmp,
    rc_in,
    r2,
    rx_in,
    r3,
    ry_in,
    relay_send,
    relay_recv,
    core_send,
    core_recv,
    y_send,
    y_recv,
    x_send,
    x_recv,
    gy_send,
    gy_recv,
    gc_send,
    gc_recv,
    rc_send,
    rc_recv,
    rx_send,
    rx_recv,
    ry_send,
    ry_recv,
):
    sections, nodes, locals_ = sizes
    across = nodes // 2
    replicas = nodes * locals_
    section = lax.axis_index("section")
    node = lax.axis_index("node")
    local = lax.axis_index("local")
    core = lax.rem(node, 2)
    column = lax.div(node, 2)
    buddy = node + 1 - 2 * core
    share = TILED // 2 // locals_
    half_rows = TILED // 2
    e_rows = OUT // replicas
    r_rows = MID // replicas
    below = (lax.rem(section + sections - 1, sections), node, local)
    above = (lax.rem(section + 1, sections), node, local)

    def y_peer(d):
        return (section, node, lax.rem(local + d, locals_))

    def x_peer(d):
        return (section, lax.rem(column + d, across) * 2 + core, local)

    other_core = (section, buddy, local)

    barrier = pltpu.get_barrier_semaphore()
    pl.semaphore_signal(barrier, inc=1, device_id=above, device_id_type=MESH)
    pl.semaphore_signal(barrier, inc=1, device_id=other_core, device_id_type=MESH)
    for d in range(1, locals_):
        pl.semaphore_signal(barrier, inc=1, device_id=y_peer(d), device_id_type=MESH)
    for d in range(1, across):
        pl.semaphore_signal(barrier, inc=1, device_id=x_peer(d), device_id_type=MESH)

    def remote(src, dst, send, recv, device):
        return pltpu.make_async_remote_copy(
            src_ref=src, dst_ref=dst, send_sem=send, recv_sem=recv, device_id=device, device_id_type=MESH
        )

    spread[...] = spread_matrix()
    pad_rows = BLOCK - ROWS
    for t in range(TICKS):
        pad = pl.ds(t * BLOCK + ROWS, pad_rows)
        x_all[pad, :] = jnp.zeros((pad_rows, OUT), BF16)
        up_all[pad, :] = jnp.zeros((pad_rows, OUT), BF16)
        cols[pad, :] = jnp.zeros((pad_rows, TAPS), BF16)
        h2_all[pad, :] = jnp.zeros((pad_rows, MID), BF16)
        ga_all[pad, :] = jnp.zeros((pad_rows, MID), BF16)
        gb_all[pad, :] = jnp.zeros((pad_rows, MID), BF16)
    for b in range(3):
        for ref in (shift, gshift):
            ref[b, :PITCH, :] = jnp.zeros((PITCH, MID), BF16)
            ref[b, PITCH + ROWS :, :] = jnp.zeros((PITCH, MID), BF16)
    prior_rs[0] = two_terms(pr_ref[...])
    prior_rs[1] = two_terms(ps_ref[...])
    prior_e[...] = two_terms(pe_ref[...])

    def rows_of(t):
        return pl.ds(t * BLOCK, ROWS)

    def block_of(t):
        return pl.ds(t * BLOCK, BLOCK)

    def forward(t):
        x_all[rows_of(t), :] = dot(spread[...], x_ref[t]).astype(BF16)
        pre1 = dot(x_all[rows_of(t), :], wr_ref[...])
        q1 = sigmoid(pre1)
        pixel = lax.broadcasted_iota(jnp.int32, (ROWS, MID), 0) % PITCH < SIDE
        slope1[...] = jnp.where(pixel, q1 * (1.0 + pre1 * (1.0 - q1)), 0.0)
        shifted_copies(pre1 * q1, shift)
        for a in range(3):
            for b in range(3):
                at = (3 * a + b) * MID
                cols[rows_of(t), at : at + MID] = shift[b, a * PITCH : a * PITCH + ROWS, :]
        pre2 = dot(cols[rows_of(t), :], ws_ref[...])
        q2 = sigmoid(pre2)
        slope2[...] = q2 * (1.0 + pre2 * (1.0 - q2))
        h2_all[rows_of(t), :] = (pre2 * q2).astype(BF16)

    def backward(t):
        up = up_all[rows_of(t), :]
        gb = (dot_t(up, we_ref[...]) * slope2[...]).astype(BF16)
        gb_all[rows_of(t), :] = gb
        shifted_copies(gb.astype(F32), gshift)
        g1 = jnp.zeros((ROWS, MID), F32)
        for a in range(3):
            for b in range(3):
                at = (3 * a + b) * MID
                moved = gshift[2 - b, (2 - a) * PITCH : (2 - a) * PITCH + ROWS, :]
                g1 = g1 + dot_t(moved, ws_ref[at : at + MID, :])
        ga = (g1 * slope1[...]).astype(BF16)
        ga_all[rows_of(t), :] = ga
        return (up.astype(F32) + dot_t(ga, wr_ref[...])).astype(BF16)

    def left_terms(t):
        a_r = two_terms(folded(dot_t(prior_rs[0], ga_all[block_of(t), :])))
        acc[:, :OUT] += dot(a_r, x_all[block_of(t), :])
        a_s = two_terms(folded(dot_t(prior_rs[1], gb_all[block_of(t), :])))
        acc[:, OUT : OUT + TAPS] += dot(a_s, cols[block_of(t), :])
        a_e = two_terms(folded(dot_t(prior_e[...], up_all[block_of(t), :])))
        acc[:, OUT + TAPS :] += dot(a_e, h2_all[block_of(t), :])

    relay = [
        remote(sent.at[t], arrived.at[t], relay_send.at[t], relay_recv.at[t], below)
        for t in range(TICKS - 1)
    ]

    forward(0)
    up_all[rows_of(0), :] = dot(spread[...], grad_ref[...]).astype(BF16)
    for t in range(TICKS):
        if t > 0:
            lossy = dot(spread[...], loss_ref[t - 1]).astype(BF16)
            relay[t - 1].wait_recv()
            last = jnp.full((ROWS, OUT), section, jnp.int32) == sections - 1
            up_all[rows_of(t), :] = jnp.where(last, lossy, arrived[t - 1])
        dx = backward(t)
        if t < TICKS - 1:
            sent[t] = dx
            if t == 0:
                pl.semaphore_wait(barrier, locals_ + across)
            relay[t].start()
            if t == 0:
                acc[:, :OUT] = dot_t(prior_rs[0], er_ref[...])
                acc[:, OUT : OUT + TAPS] = dot_t(prior_rs[1], es_ref[...])
                acc[:, OUT + TAPS :] = dot_t(prior_e[...], ee_ref[...])
            left_terms(t)
            forward(t + 1)
    left_terms(TICKS - 1)

    for j in range(COLUMNS // LANES):
        tiled[j * RANK : (j + 1) * RANK, :] = (
            acc[:RANK, j * LANES : (j + 1) * LANES] + acc[RANK:, j * LANES : (j + 1) * LANES]
        )

    mine = pl.ds(pl.multiple_of(core * half_rows, half_rows), half_rows)
    theirs = pl.ds(pl.multiple_of((1 - core) * half_rows, half_rows), half_rows)
    to_core = remote(tiled.at[theirs], core_in, core_send, core_recv, other_core)
    to_core.start()
    leaving_ref[...] = dot(gather_matrix(), dx).astype(BF16)
    to_core.wait_recv()
    half[...] = tiled[mine, :] + core_in[...]
    to_y = []
    for d in range(1, locals_):
        at = pl.multiple_of(lax.rem(local + d, locals_) * share, share)
        to_y.append(
            remote(half.at[pl.ds(at, share)], y_in.at[d - 1], y_send.at[d - 1], y_recv.at[d - 1], y_peer(d))
        )
        to_y[-1].start()
    for copy in to_y:
        copy.wait_recv()
    summed = half[pl.ds(pl.multiple_of(local * share, share), share), :]
    for d in range(locals_ - 1):
        summed = summed + y_in[d]
    own = pl.ds(pl.multiple_of(core * half_rows + local * share, share), share)
    x_own = x_in.at[0]
    x_own[...] = summed
    to_x = []
    for d in range(1, across):
        to_x.append(remote(x_own, x_in.at[d], x_send.at[d - 1], x_recv.at[d - 1], x_peer(d)))
        to_x[-1].start()
    for copy in to_x:
        copy.wait_recv()
    for d in range(1, across):
        summed = summed + x_in[d]
    full[own, :] = summed
    from_y = []
    for d in range(1, locals_):
        from_y.append(remote(full.at[own], full.at[own], gy_send.at[d - 1], gy_recv.at[d - 1], y_peer(d)))
        from_y[-1].start()
    for copy in from_y:
        copy.wait_recv()
    from_core = remote(full.at[mine], full.at[mine], gc_send, gc_recv, other_core)
    from_core.start()
    from_core.wait_recv()

    for j in range(COLUMNS // LANES):
        values = full[j * RANK : (j + 1) * RANK, :]
        high = values.astype(BF16)
        pt2[:RANK, j * LANES : (j + 1) * LANES] = high
        pt2[RANK:, j * LANES : (j + 1) * LANES] = (values - high.astype(F32)).astype(BF16)
    b_r = two_terms(folded(dot_t(pt2[:, :OUT], x_all[...])))
    sum_r = folded(dot(b_r, ga_all[...]) + dot(pt2[:, :OUT], er_ref[...]))
    b_s = two_terms(folded(dot_t(pt2[:, OUT : OUT + TAPS], cols[...])))
    sum_s = folded(dot(b_s, gb_all[...]) + dot(pt2[:, OUT : OUT + TAPS], es_ref[...]))
    b_e = two_terms(folded(dot_t(pt2[:, OUT + TAPS :], h2_all[...])))
    sum_e = folded(dot(b_e, up_all[...]) + dot(pt2[:, OUT + TAPS :], ee_ref[...]))
    right_tiles[...] = jnp.concatenate([sum_e, jnp.zeros((LANES - RANK, OUT), F32)], axis=0).T
    zero = jnp.zeros((RANK, MID), F32)
    right_tmp[...] = jnp.concatenate([zero, sum_r, sum_s, zero], axis=0).T
    for i in range(r_rows):
        right_tiles[pl.ds(i, replicas, stride=e_rows), :] += right_tmp[pl.ds(i, replicas, stride=r_rows), :]

    group = locals_ * e_rows

    def group_at(column_, core_):
        return pl.ds(pl.multiple_of((column_ * 2 + core_) * group, group), group)

    to_core2 = []
    for i in range(across):
        to_core2.append(
            remote(right_tiles.at[group_at(i, 1 - core)], rc_in.at[i], rc_send.at[i], rc_recv.at[i], other_core)
        )
        to_core2[-1].start()

    def gram(start, width):
        terms = pt2[:, start : start + width]
        products = dot_t(terms, terms)
        return (products[:RANK, :RANK] + products[RANK:, :RANK]) + (products[:RANK, RANK:] + products[RANK:, RANK:])

    row_id = lax.broadcasted_iota(jnp.int32, (RANK, RANK), 0)
    col_id = lax.broadcasted_iota(jnp.int32, (RANK, RANK), 1)
    left = [gram(*part) for part in PARTS]
    inverse = [jnp.where(row_id == col_id, 1.0, 0.0) for _ in PARTS]

    def eliminate(steps):
        for k in steps:
            for m in range(3):
                factor = left[m][:, k : k + 1] * (1.0 / left[m][k : k + 1, k : k + 1])
                factor = jnp.where(row_id[:, :1] > k, factor, 0.0)
                row_left, row_inverse = left[m][k : k + 1, :], inverse[m][k : k + 1, :]
                left[m] = left[m] - factor * row_left
                inverse[m] = inverse[m] - factor * row_inverse

    for copy in to_core2:
        copy.wait_recv()
    for i in range(across):
        r2[i] = right_tiles[group_at(i, core), :] + rc_in[i]
    to_x2 = []
    for d in range(1, across):
        to_x2.append(
            remote(r2.at[lax.rem(column + d, across)], rx_in.at[d - 1], rx_send.at[d - 1], rx_recv.at[d - 1], x_peer(d))
        )
        to_x2[-1].start()
    eliminate(range(RANK // 2))
    for copy in to_x2:
        copy.wait_recv()
    total = r2[column]
    for d in range(across - 1):
        total = total + rx_in[d]
    r3[...] = total
    to_y2 = []
    for d in range(1, locals_):
        at = pl.multiple_of(lax.rem(local + d, locals_) * e_rows, e_rows)
        to_y2.append(
            remote(r3.at[pl.ds(at, e_rows)], ry_in.at[d - 1], ry_send.at[d - 1], ry_recv.at[d - 1], y_peer(d))
        )
        to_y2[-1].start()
    eliminate(range(RANK // 2, RANK))
    for m in range(3):
        pivots = jnp.sum(jnp.where(row_id == col_id, left[m], 0.0), axis=1, keepdims=True)
        inverse[m] = inverse[m] * lax.rsqrt(pivots)

    replica = node * locals_ + local
    for m, ref in enumerate((basis_r_ref, basis_s_ref, basis_e_ref)):
        start, rows = PARTS[m]
        width = rows // replicas
        at = start + replica * width
        first = at // LANES
        tiles = 1 if LANES % width == 0 else width // LANES + 2
        pieces = []
        for i in range(tiles):
            j = jnp.minimum(first + i, COLUMNS // LANES - 1)
            pieces.append(full[pl.ds(pl.multiple_of(j * RANK, RANK), RANK), :])
        window = pieces[0] if tiles == 1 else jnp.concatenate(pieces, axis=1)
        span = tiles * LANES
        window = pltpu.roll(window, lax.rem(span - (at - first * LANES), span), 1)
        if m == 1:
            ref[...] = precise_dot(inverse[m], window)[:, :width] * math.sqrt(rows)
        else:
            ref[...] = precise_dot_t(window.T[:width, :], inverse[m]) * math.sqrt(rows)

    for copy in to_y2:
        copy.wait_recv()
    total = r3[pl.ds(pl.multiple_of(local * e_rows, e_rows), e_rows), :]
    for d in range(locals_ - 1):
        total = total + ry_in[d]
    right_e_ref[...] = precise_dot_t(total[:, :RANK], inverse[2]) / (replicas * math.sqrt(MID))
    few = total[:, RANK : 2 * RANK]
    right_r_ref[...] = precise_dot_t(few, inverse[0])[:r_rows, :] / (replicas * math.sqrt(OUT))
    few = total[:, 2 * RANK : 3 * RANK]
    right_s_ref[...] = precise_dot_t(few, inverse[1])[:r_rows, :] / (replicas * math.sqrt(TAPS))

    for copy in (*relay, to_core, *to_y, *to_x, *from_y, from_core, *to_core2, *to_x2, *to_y2):
        copy.wait_send()


def on_device(
    sizes,
    section_inputs,
    grad_in,
    loss_grad,
    w_reduce,
    w_spatial,
    w_expand,
    err_reduce,
    err_spatial,
    err_expand,
    prior_reduce,
    prior_spatial,
    prior_expand,
):
    sections, nodes, locals_ = sizes
    across = nodes // 2
    replicas = nodes * locals_
    share = TILED // 2 // locals_
    e_rows = OUT // replicas
    r_rows = MID // replicas
    group = locals_ * e_rows
    vmem = pl.BlockSpec(memory_space=pltpu.VMEM)
    dma = pltpu.SemaphoreType.DMA
    more = max(across - 1, 1)
    scratch = [
        pltpu.VMEM((ROWS, PIXELS), BF16),
        pltpu.VMEM((TICKS * BLOCK, OUT), BF16),
        pltpu.VMEM((TICKS * BLOCK, TAPS), BF16),
        pltpu.VMEM((TICKS * BLOCK, MID), BF16),
        pltpu.VMEM((TICKS * BLOCK, MID), BF16),
        pltpu.VMEM((TICKS * BLOCK, MID), BF16),
        pltpu.VMEM((TICKS * BLOCK, OUT), BF16),
        pltpu.VMEM((3, ROWS + 2 * PITCH, MID), BF16),
        pltpu.VMEM((3, ROWS + 2 * PITCH, MID), BF16),
        pltpu.VMEM((ROWS, MID), F32),
        pltpu.VMEM((ROWS, MID), F32),
        pltpu.VMEM((2, 2 * RANK, MID), BF16),
        pltpu.VMEM((2 * RANK, OUT), BF16),
        pltpu.VMEM((2 * RANK, COLUMNS), F32),
        pltpu.VMEM((TICKS - 1, ROWS, OUT), BF16),
        pltpu.VMEM((TICKS - 1, ROWS, OUT), BF16),
        pltpu.VMEM((TILED, LANES), F32),
        pltpu.VMEM((TILED // 2, LANES), F32),
        pltpu.VMEM((TILED // 2, LANES), F32),
        pltpu.VMEM((locals_ - 1, share, LANES), F32),
        pltpu.VMEM((across, share, LANES), F32),
        pltpu.VMEM((TILED, LANES), F32),
        pltpu.VMEM((2 * RANK, COLUMNS), BF16),
        pltpu.VMEM((OUT, LANES), F32),
        pltpu.VMEM((MID, LANES), F32),
        pltpu.VMEM((across, group, LANES), F32),
        pltpu.VMEM((across, group, LANES), F32),
        pltpu.VMEM((more, group, LANES), F32),
        pltpu.VMEM((group, LANES), F32),
        pltpu.VMEM((locals_ - 1, e_rows, LANES), F32),
        dma((TICKS - 1,)),
        dma((TICKS - 1,)),
        dma,
        dma,
        dma((locals_ - 1,)),
        dma((locals_ - 1,)),
        dma((more,)),
        dma((more,)),
        dma((locals_ - 1,)),
        dma((locals_ - 1,)),
        dma,
        dma,
        dma((across,)),
        dma((across,)),
        dma((more,)),
        dma((more,)),
        dma((locals_ - 1,)),
        dma((locals_ - 1,)),
    ]
    shapes = (
        jax.ShapeDtypeStruct((PIXELS, OUT), BF16),
        jax.ShapeDtypeStruct((OUT // replicas, RANK), F32),
        jax.ShapeDtypeStruct((RANK, TAPS // replicas), F32),
        jax.ShapeDtypeStruct((MID // replicas, RANK), F32),
        jax.ShapeDtypeStruct((r_rows, RANK), F32),
        jax.ShapeDtypeStruct((r_rows, RANK), F32),
        jax.ShapeDtypeStruct((e_rows, RANK), F32),
    )
    results = pl.pallas_call(
        functools.partial(kernel, sizes),
        out_shape=shapes,
        in_specs=[vmem] * 12,
        out_specs=(vmem,) * 7,
        scratch_shapes=scratch,
        compiler_params=pltpu.CompilerParams(
            collective_id=0, has_side_effects=True, vmem_limit_bytes=56 * 1024 * 1024
        ),
        cost_estimate=pl.CostEstimate(flops=5_000_000_000, bytes_accessed=6_000_000, transcendentals=500_000),
    )(
        section_inputs[0, 0],
        grad_in[0, 0],
        loss_grad[0],
        w_reduce[0],
        w_spatial[0],
        w_expand[0],
        err_reduce[0, 0],
        err_spatial[0, 0],
        err_expand[0, 0],
        prior_reduce[0],
        prior_spatial[0],
        prior_expand[0],
    )
    leaving, basis_r, basis_s, *others = results
    return (leaving[None, None], basis_r.T[None], basis_s[None], *(other.T[None] for other in others))


def solution(mesh):
    sizes = (mesh.shape["section"], mesh.shape["node"], mesh.shape["local"])
    replicas = ("node", "local")
    return jax.shard_map(
        functools.partial(on_device, sizes),
        mesh=mesh,
        in_specs=(
            P("section", replicas),
            P("section", replicas),
            P(replicas),
            P("section"),
            P("section"),
            P("section"),
            P("section", replicas),
            P("section", replicas),
            P("section", replicas),
            P("section"),
            P("section"),
            P("section"),
        ),
        out_specs=(
            P("section", replicas),
            P("section", None, replicas),
            P("section", None, replicas),
            P("section", None, replicas),
            P("section", None, replicas),
            P("section", None, replicas),
            P("section", None, replicas),
        ),
        check_vma=False,
    )
```

```python
import functools
import math

import jax
import jax.numpy as jnp
from jax import lax
from jax.experimental import pallas as pl
from jax.experimental.pallas import tpu as pltpu
from jax.sharding import PartitionSpec as P

SIDE = 14
PITCH = 16
ROWS = SIDE * PITCH
BLOCK = 256
PIXELS = SIDE * SIDE
TICKS = 4
OUT = 512
MID = 256
RANK = 32
TAPS = 9 * MID
CUTS = (0, 6, 10)
PIECES = len(CUTS)
COLUMNS = OUT + TAPS + MID
LANES = 128
TILED = COLUMNS // LANES * RANK
MESH = pl.DeviceIdType.MESH
F32 = jnp.float32
BF16 = jnp.bfloat16
PARTS = ((0, OUT), (OUT, TAPS), (OUT + TAPS, MID))


def dot(a, b):
    return jnp.dot(a, b, preferred_element_type=F32)


def dot_t(a, b):
    return lax.dot_general(a, b, (((1,), (1,)), ((), ())), preferred_element_type=F32)


def precise_dot_t(a, b):
    return lax.dot_general(
        a, b, (((1,), (1,)), ((), ())), preferred_element_type=F32, precision=lax.Precision.HIGHEST
    )


def precise_dot(a, b):
    return jnp.dot(a, b, preferred_element_type=F32, precision=lax.Precision.HIGHEST)


def two_terms(values):
    high = values.astype(BF16)
    low = (values - high.astype(F32)).astype(BF16)
    return jnp.concatenate([high, low], axis=0)


def folded(values):
    return values[:RANK] + values[RANK:]


def sigmoid(values):
    return 1.0 / (1.0 + jnp.exp(-values))


def spread_matrix():
    row = lax.broadcasted_iota(jnp.int32, (ROWS, PIXELS), 0)
    pixel = lax.broadcasted_iota(jnp.int32, (ROWS, PIXELS), 1)
    hit = ((row // PITCH) * SIDE + row % PITCH == pixel) & (row % PITCH < SIDE)
    return jnp.where(hit, 1.0, 0.0).astype(BF16)


def gather_matrix():
    row = lax.broadcasted_iota(jnp.int32, (PIXELS, ROWS), 1)
    pixel = lax.broadcasted_iota(jnp.int32, (PIXELS, ROWS), 0)
    hit = ((row // PITCH) * SIDE + row % PITCH == pixel) & (row % PITCH < SIDE)
    return jnp.where(hit, 1.0, 0.0).astype(BF16)


def shifted_copies(values, ref):
    ref[1, PITCH : PITCH + ROWS, :] = values.astype(BF16)
    ref[0, PITCH : PITCH + ROWS, :] = pltpu.roll(values, 1, 0).astype(BF16)
    ref[2, PITCH : PITCH + ROWS, :] = pltpu.roll(values, ROWS - 1, 0).astype(BF16)


def kernel(
    sizes,
    x_ref,
    grad_ref,
    loss_ref,
    wr_ref,
    ws_ref,
    we_ref,
    er_ref,
    es_ref,
    ee_ref,
    pr_ref,
    ps_ref,
    pe_ref,
    leaving_ref,
    basis_r_ref,
    basis_s_ref,
    basis_e_ref,
    right_r_ref,
    right_s_ref,
    right_e_ref,
    x,
    grad,
    loss,
    wr,
    ws,
    we,
    er,
    es,
    ee,
    spread,
    x_all,
    cols,
    h2_all,
    ga_all,
    gb_all,
    up_all,
    ws_t,
    wr_t,
    we_t,
    gcols,
    shift,
    gshift,
    slope1,
    slope2,
    prior_rs,
    prior_e,
    acc,
    sent,
    arrived,
    tiled,
    core_in,
    half,
    half_out,
    y_in,
    x_in,
    full,
    pt,
    right_tiles,
    right_tmp,
    rc_in,
    r2,
    rx_in,
    r3,
    ry_in,
    load_sem,
    relay_send,
    relay_recv,
    core_send,
    core_recv,
    y_send,
    y_recv,
    x_send,
    x_recv,
    gy_send,
    gy_recv,
    gc_send,
    gc_recv,
    rc_send,
    rc_recv,
    rx_send,
    rx_recv,
    ry_send,
    ry_recv,
):
    sections, nodes, locals_ = sizes
    across = nodes // 2
    replicas = nodes * locals_
    section = lax.axis_index("section")
    node = lax.axis_index("node")
    local = lax.axis_index("local")
    core = lax.rem(node, 2)
    column = lax.div(node, 2)
    buddy = node + 1 - 2 * core
    share = TILED // 2 // locals_
    half_rows = TILED // 2
    e_rows = OUT // replicas
    r_rows = MID // replicas
    below = (lax.rem(section + sections - 1, sections), node, local)
    above = (lax.rem(section + 1, sections), node, local)

    def y_peer(d):
        return (section, node, lax.rem(local + d, locals_))

    def x_peer(d):
        return (section, lax.rem(column + d, across) * 2 + core, local)

    other_core = (section, buddy, local)

    pairs = (
        (x_ref.at[0], x.at[0]),
        (wr_ref, wr),
        (ws_ref, ws),
        (grad_ref, grad),
        (we_ref, we),
        *((x_ref.at[t], x.at[t]) for t in range(1, TICKS)),
        (er_ref, er),
        (es_ref, es),
        (ee_ref, ee),
        (loss_ref, loss),
    )
    loads = [pltpu.make_async_copy(a, b, load_sem.at[i]) for i, (a, b) in enumerate(pairs)]
    for load in loads:
        load.start()
    barrier = pltpu.get_barrier_semaphore()
    pl.semaphore_signal(barrier, inc=1, device_id=above, device_id_type=MESH)
    pl.semaphore_signal(barrier, inc=1, device_id=other_core, device_id_type=MESH)
    for d in range(1, locals_):
        pl.semaphore_signal(barrier, inc=1, device_id=y_peer(d), device_id_type=MESH)
    for d in range(1, across):
        pl.semaphore_signal(barrier, inc=1, device_id=x_peer(d), device_id_type=MESH)

    def remote(src, dst, send, recv, device):
        return pltpu.make_async_remote_copy(
            src_ref=src, dst_ref=dst, send_sem=send, recv_sem=recv, device_id=device, device_id_type=MESH
        )

    spread[...] = spread_matrix()
    pad_rows = BLOCK - ROWS
    for t in range(TICKS):
        pad = pl.ds(t * BLOCK + ROWS, pad_rows)
        x_all[pad, :] = jnp.zeros((pad_rows, OUT), BF16)
        up_all[pad, :] = jnp.zeros((pad_rows, OUT), BF16)
        cols[pad, :] = jnp.zeros((pad_rows, TAPS), BF16)
        h2_all[pad, :] = jnp.zeros((pad_rows, MID), BF16)
        ga_all[pad, :] = jnp.zeros((pad_rows, MID), BF16)
        gb_all[pad, :] = jnp.zeros((pad_rows, MID), BF16)
    for b in range(3):
        for ref in (shift, gshift):
            ref[b, :PITCH, :] = jnp.zeros((PITCH, MID), BF16)
            ref[b, PITCH + ROWS :, :] = jnp.zeros((PITCH, MID), BF16)
    prior_rs[0] = two_terms(pr_ref[...])
    prior_rs[1] = two_terms(ps_ref[...])
    prior_e[...] = two_terms(pe_ref[...])

    def rows_of(t):
        return pl.ds(t * BLOCK, ROWS)

    def block_of(t):
        return pl.ds(t * BLOCK, BLOCK)

    def forward_one(t):
        x_all[rows_of(t), :] = dot(spread[...], x[t]).astype(BF16)
        pre1 = dot(x_all[rows_of(t), :], wr[...])
        q1 = sigmoid(pre1)
        pixel = lax.broadcasted_iota(jnp.int32, (ROWS, MID), 0) % PITCH < SIDE
        slope1[t % 2] = jnp.where(pixel, q1 * (1.0 + pre1 * (1.0 - q1)), 0.0)
        shifted_copies(pre1 * q1, shift)
        for a in range(3):
            for b in range(3):
                at = (3 * a + b) * MID
                cols[rows_of(t), at : at + MID] = shift[b, a * PITCH : a * PITCH + ROWS, :]

    def forward_two(t):
        pre2 = dot(cols[rows_of(t), :], ws[...])
        q2 = sigmoid(pre2)
        slope2[t % 2] = q2 * (1.0 + pre2 * (1.0 - q2))
        h2_all[rows_of(t), :] = (pre2 * q2).astype(BF16)

    def gb_rows(t, first, last):
        count = (last - first) * PITCH
        at = first * PITCH
        rows = pl.ds(t * BLOCK + at, count)
        if t > 0:
            is_last = jnp.full((count, OUT), section, jnp.int32) == sections - 1
            up_all[rows, :] = jnp.where(is_last, up_all[rows, :], arrived[t - 1, at : at + count, :])
        gb = (dot(up_all[rows, :], we_t[...]) * slope2[t % 2, at : at + count, :]).astype(BF16)
        gb_all[rows, :] = gb
        gb = gb.astype(F32)
        to = slice(PITCH + at, PITCH + at + count)
        gshift[1, to, :] = gb.astype(BF16)
        gshift[0, to, :] = pltpu.roll(gb, 1, 0).astype(BF16)
        gshift[2, to, :] = pltpu.roll(gb, count - 1, 0).astype(BF16)

    def ga_rows(t, first, last):
        count = (last - first) * PITCH
        at = first * PITCH
        for a in range(3):
            for b in range(3):
                tap = (3 * a + b) * MID
                gcols[at : at + count, tap : tap + MID] = gshift[
                    2 - b, (2 - a) * PITCH + at : (2 - a) * PITCH + at + count, :
                ]
        g1 = dot(gcols[at : at + count, :], ws_t[...])
        ga_all[pl.ds(t * BLOCK + at, count), :] = (g1 * slope1[t % 2, at : at + count, :]).astype(BF16)

    def dx_rows(t, first, last):
        rows = pl.ds(t * BLOCK + first * PITCH, (last - first) * PITCH)
        return (up_all[rows, :].astype(F32) + dot(ga_all[rows, :], wr_t[...])).astype(BF16)

    def left_terms(t):
        a_r = two_terms(folded(dot_t(prior_rs[0], ga_all[block_of(t), :])))
        acc[:, :OUT] += dot(a_r, x_all[block_of(t), :])
        a_s = two_terms(folded(dot_t(prior_rs[1], gb_all[block_of(t), :])))
        acc[:, OUT : OUT + TAPS] += dot(a_s, cols[block_of(t), :])
        a_e = two_terms(folded(dot_t(prior_e[...], up_all[block_of(t), :])))
        acc[:, OUT + TAPS :] += dot(a_e, h2_all[block_of(t), :])

    def piece(t, part):
        first = CUTS[part] - t if part else 0
        return first, CUTS[part + 1] - t if part < PIECES - 1 else SIDE

    relay = {}
    for t in range(TICKS - 1):
        for part in range(PIECES):
            first, last = piece(t, part)
            rows = pl.ds(first * PITCH, (last - first) * PITCH)
            sems = (relay_send.at[t, part], relay_recv.at[t, part])
            relay[t, part] = remote(sent.at[t, rows], arrived.at[t, rows], *sems, below)

    def arrive(count):
        for load in loads[arrive.done : count]:
            load.wait()
        arrive.done = count

    arrive.done = 0
    arrive(2)
    forward_one(0)
    arrive(3)
    forward_two(0)
    for k in range(9):
        ws_t[k * MID : (k + 1) * MID, :] = ws[k * MID : (k + 1) * MID, :].T
    arrive(5)
    we_t[...] = we[...].T
    wr_t[...] = wr[...].T
    up_all[rows_of(0), :] = dot(spread[...], grad[...]).astype(BF16)

    def shadow(t, part):
        if part == 0:
            arrive(8)
            forward_one(t + 1)
        elif part == 1:
            forward_two(t + 1)
        else:
            if t == 0:
                arrive(12)
                acc[:, :OUT] = dot_t(prior_rs[0], er[...])
                acc[:, OUT : OUT + TAPS] = dot_t(prior_rs[1], es[...])
                acc[:, OUT + TAPS :] = dot_t(prior_e[...], ee[...])
            up_all[rows_of(t + 1), :] = dot(spread[...], loss[t]).astype(BF16)
            left_terms(t)

    for t in range(TICKS):
        for part in range(PIECES):
            if t > 0:
                relay[t - 1, part].wait_recv()
                gb_rows(t, *piece(t - 1, part))
            elif part == 0:
                gb_rows(t, 0, SIDE)
            ga_rows(t, *piece(t, part))
            if t < TICKS - 1:
                first, last = piece(t, part)
                sent[t, first * PITCH : last * PITCH, :] = dx_rows(t, first, last)
                if t == 0 and part == 0:
                    pl.semaphore_wait(barrier, locals_ + across)
                relay[t, part].start()
                shadow(t, part)
    left_terms(TICKS - 1)

    for j in range(COLUMNS // LANES):
        tiled[j * RANK : (j + 1) * RANK, :] = (
            acc[:RANK, j * LANES : (j + 1) * LANES] + acc[RANK:, j * LANES : (j + 1) * LANES]
        )

    mine = pl.ds(pl.multiple_of(core * half_rows, half_rows), half_rows)
    theirs = pl.ds(pl.multiple_of((1 - core) * half_rows, half_rows), half_rows)
    to_core = remote(tiled.at[theirs], core_in, core_send, core_recv, other_core)
    to_core.start()
    leaving_ref[...] = dot(gather_matrix(), dx_rows(TICKS - 1, 0, SIDE)).astype(BF16)
    to_core.wait_recv()
    half[...] = tiled[mine, :] + core_in[...]
    half_out[...] = half[...].astype(BF16)
    to_y = []
    for d in range(1, locals_):
        at = pl.multiple_of(lax.rem(local + d, locals_) * share, share)
        to_y.append(
            remote(half_out.at[pl.ds(at, share)], y_in.at[d - 1], y_send.at[d - 1], y_recv.at[d - 1], y_peer(d))
        )
        to_y[-1].start()
    for copy in to_y:
        copy.wait_recv()
    summed = half[pl.ds(pl.multiple_of(local * share, share), share), :]
    for d in range(locals_ - 1):
        summed = summed + y_in[d].astype(F32)
    own = pl.ds(pl.multiple_of(core * half_rows + local * share, share), share)
    x_own = x_in.at[column]
    x_own[...] = summed
    to_x = []
    for d in range(1, across):
        to_x.append(remote(x_own, x_own, x_send.at[d - 1], x_recv.at[d - 1], x_peer(d)))
        to_x[-1].start()
    for copy in to_x:
        copy.wait_recv()
    summed = x_in[0]
    for d in range(1, across):
        summed = summed + x_in[d]
    full[own, :] = summed.astype(BF16)
    from_y = []
    for d in range(1, locals_):
        from_y.append(remote(full.at[own], full.at[own], gy_send.at[d - 1], gy_recv.at[d - 1], y_peer(d)))
        from_y[-1].start()
    for copy in from_y:
        copy.wait_recv()
    from_core = remote(full.at[mine], full.at[mine], gc_send, gc_recv, other_core)
    from_core.start()
    from_core.wait_recv()

    for j in range(COLUMNS // LANES):
        pt[:, j * LANES : (j + 1) * LANES] = full[j * RANK : (j + 1) * RANK, :]
    b_r = two_terms(dot_t(pt[:, :OUT], x_all[...]))
    sum_r = folded(dot(b_r, ga_all[...])) + dot(pt[:, :OUT], er[...])
    b_s = two_terms(dot_t(pt[:, OUT : OUT + TAPS], cols[...]))
    sum_s = folded(dot(b_s, gb_all[...])) + dot(pt[:, OUT : OUT + TAPS], es[...])
    b_e = two_terms(dot_t(pt[:, OUT + TAPS :], h2_all[...]))
    sum_e = folded(dot(b_e, up_all[...])) + dot(pt[:, OUT + TAPS :], ee[...])
    right_tiles[...] = jnp.concatenate([sum_e, jnp.zeros((LANES - RANK, OUT), F32)], axis=0).T
    zero = jnp.zeros((RANK, MID), F32)
    right_tmp[...] = jnp.concatenate([zero, sum_r, sum_s, zero], axis=0).T
    for i in range(r_rows):
        right_tiles[pl.ds(i, replicas, stride=e_rows), :] += right_tmp[pl.ds(i, replicas, stride=r_rows), :]

    group = locals_ * e_rows

    def group_at(column_, core_):
        return pl.ds(pl.multiple_of((column_ * 2 + core_) * group, group), group)

    to_core2 = []
    for i in range(across):
        to_core2.append(
            remote(right_tiles.at[group_at(i, 1 - core)], rc_in.at[i], rc_send.at[i], rc_recv.at[i], other_core)
        )
        to_core2[-1].start()

    def gram(start, width):
        terms = pt[:, start : start + width]
        return dot_t(terms, terms)

    row_id = lax.broadcasted_iota(jnp.int32, (RANK, RANK), 0)
    col_id = lax.broadcasted_iota(jnp.int32, (RANK, RANK), 1)
    left = [gram(*part) for part in PARTS]
    inverse = [jnp.where(row_id == col_id, 1.0, 0.0) for _ in PARTS]

    def eliminate(steps):
        for k in steps:
            for m in range(3):
                factor = left[m][:, k : k + 1] * (1.0 / left[m][k : k + 1, k : k + 1])
                factor = jnp.where(row_id[:, :1] > k, factor, 0.0)
                row_left, row_inverse = left[m][k : k + 1, :], inverse[m][k : k + 1, :]
                left[m] = left[m] - factor * row_left
                inverse[m] = inverse[m] - factor * row_inverse

    for copy in to_core2:
        copy.wait_recv()
    for i in range(across):
        r2[i] = right_tiles[group_at(i, core), :] + rc_in[i]
    to_x2 = []
    for d in range(1, across):
        to_x2.append(
            remote(r2.at[lax.rem(column + d, across)], rx_in.at[d - 1], rx_send.at[d - 1], rx_recv.at[d - 1], x_peer(d))
        )
        to_x2[-1].start()
    eliminate(range(RANK // 2))
    for copy in to_x2:
        copy.wait_recv()
    total = r2[column]
    for d in range(across - 1):
        total = total + rx_in[d]
    r3[...] = total
    to_y2 = []
    for d in range(1, locals_):
        at = pl.multiple_of(lax.rem(local + d, locals_) * e_rows, e_rows)
        to_y2.append(
            remote(r3.at[pl.ds(at, e_rows)], ry_in.at[d - 1], ry_send.at[d - 1], ry_recv.at[d - 1], y_peer(d))
        )
        to_y2[-1].start()
    eliminate(range(RANK // 2, RANK))
    for m in range(3):
        pivots = jnp.sum(jnp.where(row_id == col_id, left[m], 0.0), axis=1, keepdims=True)
        inverse[m] = inverse[m] * lax.rsqrt(pivots)

    replica = node * locals_ + local
    for m, ref in enumerate((basis_r_ref, basis_s_ref, basis_e_ref)):
        start, rows = PARTS[m]
        width = rows // replicas
        at = start + replica * width
        first = at // LANES
        tiles = 1 if LANES % width == 0 else width // LANES + 2
        pieces = []
        for i in range(tiles):
            j = jnp.minimum(first + i, COLUMNS // LANES - 1)
            pieces.append(full[pl.ds(pl.multiple_of(j * RANK, RANK), RANK), :].astype(F32))
        window = pieces[0] if tiles == 1 else jnp.concatenate(pieces, axis=1)
        span = tiles * LANES
        window = pltpu.roll(window, lax.rem(span - (at - first * LANES), span), 1)
        if m == 1:
            ref[...] = precise_dot(inverse[m], window)[:, :width] * math.sqrt(rows)
        else:
            ref[...] = precise_dot_t(window.T[:width, :], inverse[m]) * math.sqrt(rows)

    for copy in to_y2:
        copy.wait_recv()
    total = r3[pl.ds(pl.multiple_of(local * e_rows, e_rows), e_rows), :]
    for d in range(locals_ - 1):
        total = total + ry_in[d]
    right_e_ref[...] = precise_dot_t(total[:, :RANK], inverse[2]) / (replicas * math.sqrt(MID))
    few = total[:, RANK : 2 * RANK]
    right_r_ref[...] = precise_dot_t(few, inverse[0])[:r_rows, :] / (replicas * math.sqrt(OUT))
    few = total[:, 2 * RANK : 3 * RANK]
    right_s_ref[...] = precise_dot_t(few, inverse[1])[:r_rows, :] / (replicas * math.sqrt(TAPS))

    for copy in (*relay.values(), to_core, *to_y, *to_x, *from_y, from_core, *to_core2, *to_x2, *to_y2):
        copy.wait_send()


def hand_over(*refs):
    for source, target in zip(refs[:7], refs[7:]):
        target[...] = source[...]


def on_device(
    sizes,
    section_inputs,
    grad_in,
    loss_grad,
    w_reduce,
    w_spatial,
    w_expand,
    err_reduce,
    err_spatial,
    err_expand,
    prior_reduce,
    prior_spatial,
    prior_expand,
):
    sections, nodes, locals_ = sizes
    across = nodes // 2
    replicas = nodes * locals_
    share = TILED // 2 // locals_
    e_rows = OUT // replicas
    r_rows = MID // replicas
    group = locals_ * e_rows
    vmem = pl.BlockSpec(memory_space=pltpu.VMEM)
    dma = pltpu.SemaphoreType.DMA
    more = max(across - 1, 1)
    hbm = pl.BlockSpec(memory_space=pltpu.HBM)
    scratch = [
        pltpu.VMEM((TICKS, PIXELS, OUT), BF16),
        pltpu.VMEM((PIXELS, OUT), BF16),
        pltpu.VMEM((TICKS - 1, PIXELS, OUT), BF16),
        pltpu.VMEM((OUT, MID), BF16),
        pltpu.VMEM((TAPS, MID), BF16),
        pltpu.VMEM((MID, OUT), BF16),
        pltpu.VMEM((OUT, MID), BF16),
        pltpu.VMEM((TAPS, MID), BF16),
        pltpu.VMEM((MID, OUT), BF16),
        pltpu.VMEM((ROWS, PIXELS), BF16),
        pltpu.VMEM((TICKS * BLOCK, OUT), BF16),
        pltpu.VMEM((TICKS * BLOCK, TAPS), BF16),
        pltpu.VMEM((TICKS * BLOCK, MID), BF16),
        pltpu.VMEM((TICKS * BLOCK, MID), BF16),
        pltpu.VMEM((TICKS * BLOCK, MID), BF16),
        pltpu.VMEM((TICKS * BLOCK, OUT), BF16),
        pltpu.VMEM((TAPS, MID), BF16),
        pltpu.VMEM((MID, OUT), BF16),
        pltpu.VMEM((OUT, MID), BF16),
        pltpu.VMEM((ROWS, TAPS), BF16),
        pltpu.VMEM((3, ROWS + 2 * PITCH, MID), BF16),
        pltpu.VMEM((3, ROWS + 2 * PITCH, MID), BF16),
        pltpu.VMEM((2, ROWS, MID), F32),
        pltpu.VMEM((2, ROWS, MID), F32),
        pltpu.VMEM((2, 2 * RANK, MID), BF16),
        pltpu.VMEM((2 * RANK, OUT), BF16),
        pltpu.VMEM((2 * RANK, COLUMNS), F32),
        pltpu.VMEM((TICKS - 1, ROWS, OUT), BF16),
        pltpu.VMEM((TICKS - 1, ROWS, OUT), BF16),
        pltpu.VMEM((TILED, LANES), F32),
        pltpu.VMEM((TILED // 2, LANES), F32),
        pltpu.VMEM((TILED // 2, LANES), F32),
        pltpu.VMEM((TILED // 2, LANES), BF16),
        pltpu.VMEM((locals_ - 1, share, LANES), BF16),
        pltpu.VMEM((across, share, LANES), F32),
        pltpu.VMEM((TILED, LANES), BF16),
        pltpu.VMEM((RANK, COLUMNS), BF16),
        pltpu.VMEM((OUT, LANES), F32),
        pltpu.VMEM((MID, LANES), F32),
        pltpu.VMEM((across, group, LANES), F32),
        pltpu.VMEM((across, group, LANES), F32),
        pltpu.VMEM((more, group, LANES), F32),
        pltpu.VMEM((group, LANES), F32),
        pltpu.VMEM((locals_ - 1, e_rows, LANES), F32),
        dma((12,)),
        dma((TICKS - 1, PIECES)),
        dma((TICKS - 1, PIECES)),
        dma,
        dma,
        dma((locals_ - 1,)),
        dma((locals_ - 1,)),
        dma((more,)),
        dma((more,)),
        dma((locals_ - 1,)),
        dma((locals_ - 1,)),
        dma,
        dma,
        dma((across,)),
        dma((across,)),
        dma((more,)),
        dma((more,)),
        dma((locals_ - 1,)),
        dma((locals_ - 1,)),
    ]
    shapes = (
        jax.ShapeDtypeStruct((PIXELS, OUT), BF16),
        jax.ShapeDtypeStruct((OUT // replicas, RANK), F32),
        jax.ShapeDtypeStruct((RANK, TAPS // replicas), F32),
        jax.ShapeDtypeStruct((MID // replicas, RANK), F32),
        jax.ShapeDtypeStruct((r_rows, RANK), F32),
        jax.ShapeDtypeStruct((r_rows, RANK), F32),
        jax.ShapeDtypeStruct((e_rows, RANK), F32),
    )
    results = pl.pallas_call(
        functools.partial(kernel, sizes),
        out_shape=shapes,
        in_specs=[hbm] * 9 + [vmem] * 3,
        out_specs=(vmem,) * 7,
        scratch_shapes=scratch,
        compiler_params=pltpu.CompilerParams(
            collective_id=0, has_side_effects=True, vmem_limit_bytes=56 * 1024 * 1024
        ),
        cost_estimate=pl.CostEstimate(flops=5_000_000_000, bytes_accessed=6_000_000, transcendentals=500_000),
    )(
        section_inputs[0, 0],
        grad_in[0, 0],
        loss_grad[0],
        w_reduce[0],
        w_spatial[0],
        w_expand[0],
        err_reduce[0, 0],
        err_spatial[0, 0],
        err_expand[0, 0],
        prior_reduce[0],
        prior_spatial[0],
        prior_expand[0],
    )
    leaving, basis_r, basis_s, *others = pl.pallas_call(
        hand_over, out_shape=shapes, in_specs=[vmem] * 7, out_specs=(vmem,) * 7
    )(*results)
    return (leaving[None, None], basis_r.T[None], basis_s[None], *(other.T[None] for other in others))


def solution(mesh):
    sizes = (mesh.shape["section"], mesh.shape["node"], mesh.shape["local"])
    replicas = ("node", "local")
    return jax.shard_map(
        functools.partial(on_device, sizes),
        mesh=mesh,
        in_specs=(
            P("section", replicas),
            P("section", replicas),
            P(replicas),
            P("section"),
            P("section"),
            P("section"),
            P("section", replicas),
            P("section", replicas),
            P("section", replicas),
            P("section"),
            P("section"),
            P("section"),
        ),
        out_specs=(
            P("section", replicas),
            P("section", None, replicas),
            P("section", None, replicas),
            P("section", None, replicas),
            P("section", None, replicas),
            P("section", None, replicas),
            P("section", None, replicas),
        ),
        check_vma=False,
    )
```

```python
import functools
import math

import jax
import jax.numpy as jnp
from jax import lax
from jax.experimental import pallas as pl
from jax.experimental.pallas import tpu as pltpu
from jax.sharding import PartitionSpec as P

SIDE = 14
PITCH = 16
ROWS = SIDE * PITCH
BLOCK = 256
PIXELS = SIDE * SIDE
TICKS = 4
OUT = 512
MID = 256
RANK = 32
TAPS = 9 * MID
CUTS = (0, 6, 10)
PIECES = len(CUTS)
COLUMNS = OUT + TAPS + MID
LANES = 128
TILED = COLUMNS // LANES * RANK
MESH = pl.DeviceIdType.MESH
F32 = jnp.float32
BF16 = jnp.bfloat16
PARTS = ((0, OUT), (OUT, TAPS), (OUT + TAPS, MID))


HALF_TILES = COLUMNS // LANES // 2
HALVES = ((0, OUT // 2), (OUT, TAPS // 2), (OUT + TAPS, MID // 2))
LATE_TILES = OUT // 2 // LANES


def tile_place(tile):
    place = 0
    for start, width in HALVES:
        first, count = start // LANES, width // LANES
        for half in range(2):
            inside = (tile >= first + half * count) & (tile < first + (half + 1) * count)
            here = half * HALF_TILES + place + tile - first - half * count
            yield inside, here
        place += count


def placed(tile):
    if isinstance(tile, int):
        return next(here for inside, here in tile_place(tile) if inside)
    at = 0
    for inside, here in tile_place(tile):
        at = jnp.where(inside, here, at)
    return at


def dot(a, b):
    return jnp.dot(a, b, preferred_element_type=F32)


def dot_t(a, b):
    return lax.dot_general(a, b, (((1,), (1,)), ((), ())), preferred_element_type=F32)


def precise_dot_t(a, b):
    return lax.dot_general(
        a, b, (((1,), (1,)), ((), ())), preferred_element_type=F32, precision=lax.Precision.HIGHEST
    )


def precise_dot(a, b):
    return jnp.dot(a, b, preferred_element_type=F32, precision=lax.Precision.HIGHEST)


def two_terms(values):
    high = values.astype(BF16)
    low = (values - high.astype(F32)).astype(BF16)
    return jnp.concatenate([high, low], axis=0)


def folded(values):
    return values[:RANK] + values[RANK:]


def sigmoid(values):
    return 1.0 / (1.0 + jnp.exp(-values))


def spread_matrix():
    row = lax.broadcasted_iota(jnp.int32, (ROWS, PIXELS), 0)
    pixel = lax.broadcasted_iota(jnp.int32, (ROWS, PIXELS), 1)
    hit = ((row // PITCH) * SIDE + row % PITCH == pixel) & (row % PITCH < SIDE)
    return jnp.where(hit, 1.0, 0.0).astype(BF16)


def gather_matrix():
    row = lax.broadcasted_iota(jnp.int32, (PIXELS, ROWS), 1)
    pixel = lax.broadcasted_iota(jnp.int32, (PIXELS, ROWS), 0)
    hit = ((row // PITCH) * SIDE + row % PITCH == pixel) & (row % PITCH < SIDE)
    return jnp.where(hit, 1.0, 0.0).astype(BF16)


def shifted_copies(values, ref):
    ref[1, PITCH : PITCH + ROWS, :] = values.astype(BF16)
    ref[0, PITCH : PITCH + ROWS, :] = pltpu.roll(values, 1, 0).astype(BF16)
    ref[2, PITCH : PITCH + ROWS, :] = pltpu.roll(values, ROWS - 1, 0).astype(BF16)


def kernel(
    sizes,
    x_ref,
    grad_ref,
    loss_ref,
    wr_ref,
    ws_ref,
    we_ref,
    er_ref,
    es_ref,
    ee_ref,
    pr_ref,
    ps_ref,
    pe_ref,
    leaving_ref,
    basis_r_ref,
    basis_s_ref,
    basis_e_ref,
    right_r_ref,
    right_s_ref,
    right_e_ref,
    x,
    grad,
    loss,
    wr,
    ws,
    we,
    er,
    es,
    ee,
    spread,
    x_all,
    cols,
    h2_all,
    ga_all,
    gb_all,
    up_all,
    ws_t,
    wr_t,
    we_t,
    gcols,
    shift,
    gshift,
    slope1,
    slope2,
    prior_rs,
    prior_e,
    acc,
    sent,
    arrived,
    tiled,
    core_in,
    half,
    half_out,
    y_in,
    x_in,
    full,
    right_tiles,
    right_tmp,
    rc_in,
    r2,
    ry_in,
    load_sem,
    relay_send,
    relay_recv,
    core_send,
    core_recv,
    y_send,
    y_recv,
    x_send,
    x_recv,
    gy_send,
    gy_recv,
    gc_send,
    gc_recv,
    rc_send,
    rc_recv,
    ry_send,
    ry_recv,
):
    sections, nodes, locals_ = sizes
    across = nodes // 2
    replicas = nodes * locals_
    section = lax.axis_index("section")
    node = lax.axis_index("node")
    local = lax.axis_index("local")
    core = lax.rem(node, 2)
    column = lax.div(node, 2)
    buddy = node + 1 - 2 * core
    share = TILED // 2 // locals_
    half_rows = TILED // 2
    e_rows = OUT // replicas
    r_rows = MID // replicas
    below = (lax.rem(section + sections - 1, sections), node, local)
    above = (lax.rem(section + 1, sections), node, local)

    def y_peer(d):
        return (section, node, lax.rem(local + d, locals_))

    def x_peer(d):
        return (section, lax.rem(column + d, across) * 2 + core, local)

    def plane_peer(dx, dy):
        return (section, lax.rem(column + dx, across) * 2 + core, lax.rem(local + dy, locals_))

    other_core = (section, buddy, local)

    pairs = (
        (x_ref.at[0], x.at[0]),
        (wr_ref, wr),
        (ws_ref, ws),
        (grad_ref, grad),
        (we_ref, we),
        *((x_ref.at[t], x.at[t]) for t in range(1, TICKS)),
        (er_ref, er),
        (es_ref, es),
        (ee_ref, ee),
        (loss_ref, loss),
    )
    loads = [pltpu.make_async_copy(a, b, load_sem.at[i]) for i, (a, b) in enumerate(pairs)]
    for load in loads:
        load.start()
    barrier = pltpu.get_barrier_semaphore()
    pl.semaphore_signal(barrier, inc=1, device_id=above, device_id_type=MESH)
    pl.semaphore_signal(barrier, inc=1, device_id=other_core, device_id_type=MESH)
    for d in range(1, locals_):
        pl.semaphore_signal(barrier, inc=1, device_id=y_peer(d), device_id_type=MESH)
    for d in range(1, across):
        pl.semaphore_signal(barrier, inc=1, device_id=x_peer(d), device_id_type=MESH)
    for dx in range(1, across):
        for dy in range(1, locals_):
            pl.semaphore_signal(barrier, inc=1, device_id=plane_peer(dx, dy), device_id_type=MESH)

    def remote(src, dst, send, recv, device):
        return pltpu.make_async_remote_copy(
            src_ref=src, dst_ref=dst, send_sem=send, recv_sem=recv, device_id=device, device_id_type=MESH
        )

    spread[...] = spread_matrix()
    pad_rows = BLOCK - ROWS
    for t in range(TICKS):
        pad = pl.ds(t * BLOCK + ROWS, pad_rows)
        x_all[pad, :] = jnp.zeros((pad_rows, OUT), BF16)
        up_all[pad, :] = jnp.zeros((pad_rows, OUT), BF16)
        cols[pad, :] = jnp.zeros((pad_rows, TAPS), BF16)
        h2_all[pad, :] = jnp.zeros((pad_rows, MID), BF16)
        ga_all[pad, :] = jnp.zeros((pad_rows, MID), BF16)
        gb_all[pad, :] = jnp.zeros((pad_rows, MID), BF16)
    for b in range(3):
        for ref in (shift, gshift):
            ref[b, :PITCH, :] = jnp.zeros((PITCH, MID), BF16)
            ref[b, PITCH + ROWS :, :] = jnp.zeros((PITCH, MID), BF16)
    prior_rs[0] = two_terms(pr_ref[...])
    prior_rs[1] = two_terms(ps_ref[...])
    prior_e[...] = two_terms(pe_ref[...])

    def rows_of(t):
        return pl.ds(t * BLOCK, ROWS)

    def block_of(t):
        return pl.ds(t * BLOCK, BLOCK)

    def forward_one(t):
        x_all[rows_of(t), :] = dot(spread[...], x[t]).astype(BF16)
        pre1 = dot(x_all[rows_of(t), :], wr[...])
        q1 = sigmoid(pre1)
        pixel = lax.broadcasted_iota(jnp.int32, (ROWS, MID), 0) % PITCH < SIDE
        slope1[t % 2] = jnp.where(pixel, q1 * (1.0 + pre1 * (1.0 - q1)), 0.0)
        shifted_copies(pre1 * q1, shift)
        for a in range(3):
            for b in range(3):
                at = (3 * a + b) * MID
                cols[rows_of(t), at : at + MID] = shift[b, a * PITCH : a * PITCH + ROWS, :]

    def forward_two(t):
        pre2 = dot(cols[rows_of(t), :], ws[...])
        q2 = sigmoid(pre2)
        slope2[t % 2] = q2 * (1.0 + pre2 * (1.0 - q2))
        h2_all[rows_of(t), :] = (pre2 * q2).astype(BF16)

    def gb_rows(t, first, last):
        count = (last - first) * PITCH
        at = first * PITCH
        rows = pl.ds(t * BLOCK + at, count)
        if t > 0:
            is_last = jnp.full((count, OUT), section, jnp.int32) == sections - 1
            up_all[rows, :] = jnp.where(is_last, up_all[rows, :], arrived[t - 1, at : at + count, :])
        gb = (dot(up_all[rows, :], we_t[...]) * slope2[t % 2, at : at + count, :]).astype(BF16)
        gb_all[rows, :] = gb
        gb = gb.astype(F32)
        to = slice(PITCH + at, PITCH + at + count)
        gshift[1, to, :] = gb.astype(BF16)
        gshift[0, to, :] = pltpu.roll(gb, 1, 0).astype(BF16)
        gshift[2, to, :] = pltpu.roll(gb, count - 1, 0).astype(BF16)

    def ga_rows(t, first, last):
        count = (last - first) * PITCH
        at = first * PITCH
        for a in range(3):
            for b in range(3):
                tap = (3 * a + b) * MID
                gcols[at : at + count, tap : tap + MID] = gshift[
                    2 - b, (2 - a) * PITCH + at : (2 - a) * PITCH + at + count, :
                ]
        g1 = dot(gcols[at : at + count, :], ws_t[...])
        ga_all[pl.ds(t * BLOCK + at, count), :] = (g1 * slope1[t % 2, at : at + count, :]).astype(BF16)

    def dx_rows(t, first, last):
        rows = pl.ds(t * BLOCK + first * PITCH, (last - first) * PITCH)
        return (up_all[rows, :].astype(F32) + dot(ga_all[rows, :], wr_t[...])).astype(BF16)

    def left_late(t):
        a_r = two_terms(folded(dot_t(prior_rs[0], ga_all[block_of(t), :])))
        acc[:, :OUT] += dot(a_r, x_all[block_of(t), :])

    def left_early(t):
        a_s = two_terms(folded(dot_t(prior_rs[1], gb_all[block_of(t), :])))
        acc[:, OUT : OUT + TAPS] += dot(a_s, cols[block_of(t), :])
        a_e = two_terms(folded(dot_t(prior_e[...], up_all[block_of(t), :])))
        acc[:, OUT + TAPS :] += dot(a_e, h2_all[block_of(t), :])

    def fill(tiles):
        for j in tiles:
            at = placed(j) * RANK
            tiled[at : at + RANK, :] = (
                acc[:RANK, j * LANES : (j + 1) * LANES] + acc[RANK:, j * LANES : (j + 1) * LANES]
            )

    def piece(t, part):
        first = CUTS[part] - t if part else 0
        return first, CUTS[part + 1] - t if part < PIECES - 1 else SIDE

    relay = {}
    for t in range(TICKS - 1):
        for part in range(PIECES):
            first, last = piece(t, part)
            rows = pl.ds(first * PITCH, (last - first) * PITCH)
            sems = (relay_send.at[t, part], relay_recv.at[t, part])
            relay[t, part] = remote(sent.at[t, rows], arrived.at[t, rows], *sems, below)

    def arrive(count):
        for load in loads[arrive.done : count]:
            load.wait()
        arrive.done = count

    arrive.done = 0
    arrive(2)
    forward_one(0)
    arrive(3)
    forward_two(0)
    for k in range(9):
        ws_t[k * MID : (k + 1) * MID, :] = ws[k * MID : (k + 1) * MID, :].T
    arrive(5)
    we_t[...] = we[...].T
    wr_t[...] = wr[...].T
    up_all[rows_of(0), :] = dot(spread[...], grad[...]).astype(BF16)

    def shadow(t, part):
        if part == 0:
            arrive(8)
            forward_one(t + 1)
        elif part == 1:
            forward_two(t + 1)
        else:
            if t == 0:
                arrive(12)
                acc[:, :OUT] = dot_t(prior_rs[0], er[...])
                acc[:, OUT : OUT + TAPS] = dot_t(prior_rs[1], es[...])
                acc[:, OUT + TAPS :] = dot_t(prior_e[...], ee[...])
            up_all[rows_of(t + 1), :] = dot(spread[...], loss[t]).astype(BF16)
            left_late(t)
            left_early(t)

    mine = pl.ds(pl.multiple_of(core * half_rows, half_rows), half_rows)
    late = LATE_TILES * RANK
    to_core = []
    for i, (first, count) in enumerate(((late, half_rows - late), (0, late))):
        theirs = pl.ds(pl.multiple_of((1 - core) * half_rows + first, RANK), count)
        there = core_in.at[first : first + count]
        to_core.append(remote(tiled.at[theirs], there, core_send.at[i], core_recv.at[i], other_core))

    for t in range(TICKS):
        for part in range(PIECES):
            if t > 0:
                relay[t - 1, part].wait_recv()
                gb_rows(t, *piece(t - 1, part))
            elif part == 0:
                gb_rows(t, 0, SIDE)
            if t == TICKS - 1 and part == PIECES - 1:
                left_early(t)
                fill(range(OUT // LANES, COLUMNS // LANES))
                to_core[0].start()
            ga_rows(t, *piece(t, part))
            if t < TICKS - 1:
                first, last = piece(t, part)
                sent[t, first * PITCH : last * PITCH, :] = dx_rows(t, first, last)
                if t == 0 and part == 0:
                    pl.semaphore_wait(barrier, locals_ * across + 1)
                relay[t, part].start()
                shadow(t, part)
    left_late(TICKS - 1)
    fill(range(OUT // LANES))
    to_core[1].start()
    leaving_ref[...] = dot(gather_matrix(), dx_rows(TICKS - 1, 0, SIDE)).astype(BF16)
    for copy in to_core:
        copy.wait_recv()
    half[...] = tiled[mine, :] + core_in[...]
    half_out[...] = half[...].astype(BF16)
    to_y = []
    for d in range(1, locals_):
        at = pl.multiple_of(lax.rem(local + d, locals_) * share, share)
        to_y.append(
            remote(half_out.at[pl.ds(at, share)], y_in.at[d - 1], y_send.at[d - 1], y_recv.at[d - 1], y_peer(d))
        )
        to_y[-1].start()
    for copy in to_y:
        copy.wait_recv()
    summed = half[pl.ds(pl.multiple_of(local * share, share), share), :]
    for d in range(locals_ - 1):
        summed = summed + y_in[d].astype(F32)
    own = pl.ds(pl.multiple_of(core * half_rows + local * share, share), share)
    x_own = x_in.at[column]
    x_own[...] = summed
    to_x = []
    for d in range(1, across):
        to_x.append(remote(x_own, x_own, x_send.at[d - 1], x_recv.at[d - 1], x_peer(d)))
        to_x[-1].start()
    for copy in to_x:
        copy.wait_recv()
    summed = x_in[0]
    for d in range(1, across):
        summed = summed + x_in[d]
    full[own, :] = summed.astype(BF16)
    from_y = []
    for d in range(1, locals_):
        from_y.append(remote(full.at[own], full.at[own], gy_send.at[d - 1], gy_recv.at[d - 1], y_peer(d)))
        from_y[-1].start()
    for copy in from_y:
        copy.wait_recv()
    from_core = remote(full.at[mine], full.at[mine], gc_send, gc_recv, other_core)
    from_core.start()

    def half_products(which):
        tiles = []
        for i in range(HALF_TILES):
            at = pl.multiple_of(which * half_rows + i * RANK, RANK)
            tiles.append(full[pl.ds(at, RANK), :])
        results = []
        first = 0
        for (_, width), inputs, errors in zip(HALVES, (x_all, cols, h2_all), (er, es, ee)):
            terms = jnp.concatenate(tiles[first : first + width // LANES], axis=1)
            first += width // LANES
            span = pl.ds(pl.multiple_of(which * width, LANES), width)
            results += [dot_t(terms, inputs[:, span]), dot(terms, errors[span, :]), dot_t(terms, terms)]
        return results

    products = half_products(core)
    from_core.wait_recv()
    products = [a + b for a, b in zip(products, half_products(1 - core))]
    sum_r = folded(dot(two_terms(products[0]), ga_all[...])) + products[1]
    sum_s = folded(dot(two_terms(products[3]), gb_all[...])) + products[4]
    sum_e = folded(dot(two_terms(products[6]), up_all[...])) + products[7]
    right_tiles[...] = jnp.concatenate([sum_e, jnp.zeros((LANES - RANK, OUT), F32)], axis=0).T
    zero = jnp.zeros((RANK, MID), F32)
    right_tmp[...] = jnp.concatenate([zero, sum_r, sum_s, zero], axis=0).T
    for i in range(r_rows):
        right_tiles[pl.ds(i, replicas, stride=e_rows), :] += right_tmp[pl.ds(i, replicas, stride=r_rows), :]

    group = locals_ * e_rows

    def group_at(column_, core_):
        return pl.ds(pl.multiple_of((column_ * 2 + core_) * group, group), group)

    to_core2 = []
    for i in range(across):
        to_core2.append(
            remote(right_tiles.at[group_at(i, 1 - core)], rc_in.at[i], rc_send.at[i], rc_recv.at[i], other_core)
        )
        to_core2[-1].start()

    row_id = lax.broadcasted_iota(jnp.int32, (RANK, RANK), 0)
    col_id = lax.broadcasted_iota(jnp.int32, (RANK, RANK), 1)
    left = [products[2], products[5], products[8]]
    inverse = [jnp.where(row_id == col_id, 1.0, 0.0) for _ in PARTS]

    def eliminate(steps):
        for k in steps:
            for m in range(3):
                factor = left[m][:, k : k + 1] * (1.0 / left[m][k : k + 1, k : k + 1])
                factor = jnp.where(row_id[:, :1] > k, factor, 0.0)
                row_left, row_inverse = left[m][k : k + 1, :], inverse[m][k : k + 1, :]
                left[m] = left[m] - factor * row_left
                inverse[m] = inverse[m] - factor * row_inverse

    for copy in to_core2:
        copy.wait_recv()
    for i in range(across):
        r2[i] = right_tiles[group_at(i, core), :] + rc_in[i]
    to_plane = []
    for dx in range(across):
        for dy in range(locals_):
            if dx + dy > 0:
                at = pl.multiple_of(lax.rem(local + dy, locals_) * e_rows, e_rows)
                source = r2.at[lax.rem(column + dx, across), pl.ds(at, e_rows)]
                slot = dx * locals_ + dy - 1
                sems = (ry_send.at[slot], ry_recv.at[slot])
                to_plane.append(remote(source, ry_in.at[slot], *sems, plane_peer(dx, dy)))
                to_plane[-1].start()
    eliminate(range(RANK))
    for m in range(3):
        pivots = jnp.sum(jnp.where(row_id == col_id, left[m], 0.0), axis=1, keepdims=True)
        inverse[m] = inverse[m] * lax.rsqrt(pivots)

    replica = node * locals_ + local
    for m, ref in enumerate((basis_r_ref, basis_s_ref, basis_e_ref)):
        start, rows = PARTS[m]
        width = rows // replicas
        at = start + replica * width
        first = at // LANES
        tiles = 1 if LANES % width == 0 else width // LANES + 2
        pieces = []
        for i in range(tiles):
            j = jnp.minimum(first + i, COLUMNS // LANES - 1)
            pieces.append(full[pl.ds(pl.multiple_of(placed(j) * RANK, RANK), RANK), :].astype(F32))
        window = pieces[0] if tiles == 1 else jnp.concatenate(pieces, axis=1)
        span = tiles * LANES
        window = pltpu.roll(window, lax.rem(span - (at - first * LANES), span), 1)
        if m == 1:
            ref[...] = precise_dot(inverse[m], window)[:, :width] * math.sqrt(rows)
        else:
            ref[...] = precise_dot_t(window.T[:width, :], inverse[m]) * math.sqrt(rows)

    for copy in to_plane:
        copy.wait_recv()
    total = r2[column, pl.ds(pl.multiple_of(local * e_rows, e_rows), e_rows), :]
    for slot in range(across * locals_ - 1):
        total = total + ry_in[slot]
    right_e_ref[...] = precise_dot_t(total[:, :RANK], inverse[2]) / (replicas * math.sqrt(MID))
    few = total[:, RANK : 2 * RANK]
    right_r_ref[...] = precise_dot_t(few, inverse[0])[:r_rows, :] / (replicas * math.sqrt(OUT))
    few = total[:, 2 * RANK : 3 * RANK]
    right_s_ref[...] = precise_dot_t(few, inverse[1])[:r_rows, :] / (replicas * math.sqrt(TAPS))

    for copy in (*relay.values(), *to_core, *to_y, *to_x, *from_y, from_core, *to_core2, *to_plane):
        copy.wait_send()


def hand_over(*refs):
    for source, target in zip(refs[:7], refs[7:]):
        target[...] = source[...]


def on_device(
    sizes,
    section_inputs,
    grad_in,
    loss_grad,
    w_reduce,
    w_spatial,
    w_expand,
    err_reduce,
    err_spatial,
    err_expand,
    prior_reduce,
    prior_spatial,
    prior_expand,
):
    sections, nodes, locals_ = sizes
    across = nodes // 2
    replicas = nodes * locals_
    share = TILED // 2 // locals_
    e_rows = OUT // replicas
    r_rows = MID // replicas
    group = locals_ * e_rows
    vmem = pl.BlockSpec(memory_space=pltpu.VMEM)
    dma = pltpu.SemaphoreType.DMA
    more = max(across - 1, 1)
    hbm = pl.BlockSpec(memory_space=pltpu.HBM)
    scratch = [
        pltpu.VMEM((TICKS, PIXELS, OUT), BF16),
        pltpu.VMEM((PIXELS, OUT), BF16),
        pltpu.VMEM((TICKS - 1, PIXELS, OUT), BF16),
        pltpu.VMEM((OUT, MID), BF16),
        pltpu.VMEM((TAPS, MID), BF16),
        pltpu.VMEM((MID, OUT), BF16),
        pltpu.VMEM((OUT, MID), BF16),
        pltpu.VMEM((TAPS, MID), BF16),
        pltpu.VMEM((MID, OUT), BF16),
        pltpu.VMEM((ROWS, PIXELS), BF16),
        pltpu.VMEM((TICKS * BLOCK, OUT), BF16),
        pltpu.VMEM((TICKS * BLOCK, TAPS), BF16),
        pltpu.VMEM((TICKS * BLOCK, MID), BF16),
        pltpu.VMEM((TICKS * BLOCK, MID), BF16),
        pltpu.VMEM((TICKS * BLOCK, MID), BF16),
        pltpu.VMEM((TICKS * BLOCK, OUT), BF16),
        pltpu.VMEM((TAPS, MID), BF16),
        pltpu.VMEM((MID, OUT), BF16),
        pltpu.VMEM((OUT, MID), BF16),
        pltpu.VMEM((ROWS, TAPS), BF16),
        pltpu.VMEM((3, ROWS + 2 * PITCH, MID), BF16),
        pltpu.VMEM((3, ROWS + 2 * PITCH, MID), BF16),
        pltpu.VMEM((2, ROWS, MID), F32),
        pltpu.VMEM((2, ROWS, MID), F32),
        pltpu.VMEM((2, 2 * RANK, MID), BF16),
        pltpu.VMEM((2 * RANK, OUT), BF16),
        pltpu.VMEM((2 * RANK, COLUMNS), F32),
        pltpu.VMEM((TICKS - 1, ROWS, OUT), BF16),
        pltpu.VMEM((TICKS - 1, ROWS, OUT), BF16),
        pltpu.VMEM((TILED, LANES), F32),
        pltpu.VMEM((TILED // 2, LANES), F32),
        pltpu.VMEM((TILED // 2, LANES), F32),
        pltpu.VMEM((TILED // 2, LANES), BF16),
        pltpu.VMEM((locals_ - 1, share, LANES), BF16),
        pltpu.VMEM((across, share, LANES), F32),
        pltpu.VMEM((TILED, LANES), BF16),
        pltpu.VMEM((OUT, LANES), F32),
        pltpu.VMEM((MID, LANES), F32),
        pltpu.VMEM((across, group, LANES), F32),
        pltpu.VMEM((across, group, LANES), F32),
        pltpu.VMEM((across * locals_ - 1, e_rows, LANES), F32),
        dma((12,)),
        dma((TICKS - 1, PIECES)),
        dma((TICKS - 1, PIECES)),
        dma((2,)),
        dma((2,)),
        dma((locals_ - 1,)),
        dma((locals_ - 1,)),
        dma((more,)),
        dma((more,)),
        dma((locals_ - 1,)),
        dma((locals_ - 1,)),
        dma,
        dma,
        dma((across,)),
        dma((across,)),
        dma((across * locals_ - 1,)),
        dma((across * locals_ - 1,)),
    ]
    shapes = (
        jax.ShapeDtypeStruct((PIXELS, OUT), BF16),
        jax.ShapeDtypeStruct((OUT // replicas, RANK), F32),
        jax.ShapeDtypeStruct((RANK, TAPS // replicas), F32),
        jax.ShapeDtypeStruct((MID // replicas, RANK), F32),
        jax.ShapeDtypeStruct((r_rows, RANK), F32),
        jax.ShapeDtypeStruct((r_rows, RANK), F32),
        jax.ShapeDtypeStruct((e_rows, RANK), F32),
    )
    results = pl.pallas_call(
        functools.partial(kernel, sizes),
        out_shape=shapes,
        in_specs=[hbm] * 9 + [vmem] * 3,
        out_specs=(vmem,) * 7,
        scratch_shapes=scratch,
        compiler_params=pltpu.CompilerParams(
            collective_id=0, has_side_effects=True, vmem_limit_bytes=56 * 1024 * 1024
        ),
        cost_estimate=pl.CostEstimate(flops=5_000_000_000, bytes_accessed=6_000_000, transcendentals=500_000),
    )(
        section_inputs[0, 0],
        grad_in[0, 0],
        loss_grad[0],
        w_reduce[0],
        w_spatial[0],
        w_expand[0],
        err_reduce[0, 0],
        err_spatial[0, 0],
        err_expand[0, 0],
        prior_reduce[0],
        prior_spatial[0],
        prior_expand[0],
    )
    leaving, basis_r, basis_s, *others = pl.pallas_call(
        hand_over, out_shape=shapes, in_specs=[vmem] * 7, out_specs=(vmem,) * 7
    )(*results)
    return (leaving[None, None], basis_r.T[None], basis_s[None], *(other.T[None] for other in others))


def solution(mesh):
    sizes = (mesh.shape["section"], mesh.shape["node"], mesh.shape["local"])
    replicas = ("node", "local")
    return jax.shard_map(
        functools.partial(on_device, sizes),
        mesh=mesh,
        in_specs=(
            P("section", replicas),
            P("section", replicas),
            P(replicas),
            P("section"),
            P("section"),
            P("section"),
            P("section", replicas),
            P("section", replicas),
            P("section", replicas),
            P("section"),
            P("section"),
            P("section"),
        ),
        out_specs=(
            P("section", replicas),
            P("section", None, replicas),
            P("section", None, replicas),
            P("section", None, replicas),
            P("section", None, replicas),
            P("section", None, replicas),
            P("section", None, replicas),
        ),
        check_vma=False,
    )
```

```python
import functools
import math

import jax
import jax.numpy as jnp
from jax import lax
from jax.experimental import pallas as pl
from jax.experimental.pallas import tpu as pltpu
from jax.sharding import PartitionSpec as P

SIDE = 14
PITCH = 16
ROWS = SIDE * PITCH
BLOCK = 256
PIXELS = SIDE * SIDE
TICKS = 4
OUT = 512
MID = 256
RANK = 32
TAPS = 9 * MID
CUTS = (0, 6, 10)
PIECES = len(CUTS)
COLUMNS = OUT + TAPS + MID
LANES = 128
TILED = COLUMNS // LANES * RANK
MESH = pl.DeviceIdType.MESH
F32 = jnp.float32
BF16 = jnp.bfloat16
PARTS = ((0, OUT), (OUT, TAPS), (OUT + TAPS, MID))


HALF_TILES = COLUMNS // LANES // 2
HALVES = ((0, OUT // 2), (OUT, TAPS // 2), (OUT + TAPS, MID // 2))
LATE_TILES = OUT // 2 // LANES


def tile_place(tile):
    place = 0
    for start, width in HALVES:
        first, count = start // LANES, width // LANES
        for half in range(2):
            inside = (tile >= first + half * count) & (tile < first + (half + 1) * count)
            here = half * HALF_TILES + place + tile - first - half * count
            yield inside, here
        place += count


def placed(tile):
    if isinstance(tile, int):
        return next(here for inside, here in tile_place(tile) if inside)
    at = 0
    for inside, here in tile_place(tile):
        at = jnp.where(inside, here, at)
    return at


def dot(a, b):
    return jnp.dot(a, b, preferred_element_type=F32)


def dot_t(a, b):
    return lax.dot_general(a, b, (((1,), (1,)), ((), ())), preferred_element_type=F32)


def precise_dot_t(a, b):
    return lax.dot_general(
        a, b, (((1,), (1,)), ((), ())), preferred_element_type=F32, precision=lax.Precision.HIGHEST
    )


def precise_dot(a, b):
    return jnp.dot(a, b, preferred_element_type=F32, precision=lax.Precision.HIGHEST)


def two_terms(values):
    high = values.astype(BF16)
    low = (values - high.astype(F32)).astype(BF16)
    return jnp.concatenate([high, low], axis=0)


def folded(values):
    return values[:RANK] + values[RANK:]


def sigmoid(values):
    return 1.0 / (1.0 + jnp.exp(-values))


def spread_matrix():
    row = lax.broadcasted_iota(jnp.int32, (ROWS, PIXELS), 0)
    pixel = lax.broadcasted_iota(jnp.int32, (ROWS, PIXELS), 1)
    hit = ((row // PITCH) * SIDE + row % PITCH == pixel) & (row % PITCH < SIDE)
    return jnp.where(hit, 1.0, 0.0).astype(BF16)


def gather_matrix():
    row = lax.broadcasted_iota(jnp.int32, (PIXELS, ROWS), 1)
    pixel = lax.broadcasted_iota(jnp.int32, (PIXELS, ROWS), 0)
    hit = ((row // PITCH) * SIDE + row % PITCH == pixel) & (row % PITCH < SIDE)
    return jnp.where(hit, 1.0, 0.0).astype(BF16)


def shifted_copies(values, ref):
    ref[1, PITCH : PITCH + ROWS, :] = values.astype(BF16)
    ref[0, PITCH : PITCH + ROWS, :] = pltpu.roll(values, 1, 0).astype(BF16)
    ref[2, PITCH : PITCH + ROWS, :] = pltpu.roll(values, ROWS - 1, 0).astype(BF16)


def kernel(
    sizes,
    x_ref,
    grad_ref,
    loss_ref,
    wr_ref,
    ws_ref,
    we_ref,
    er_ref,
    es_ref,
    ee_ref,
    pr_ref,
    ps_ref,
    pe_ref,
    leaving_ref,
    basis_r_ref,
    basis_s_ref,
    basis_e_ref,
    right_r_ref,
    right_s_ref,
    right_e_ref,
    x,
    grad,
    loss,
    wr,
    ws,
    we,
    er,
    es,
    ee,
    spread,
    x_all,
    cols,
    h2_all,
    ga_all,
    gb_all,
    up_all,
    ws_t,
    wr_t,
    we_t,
    gcols,
    shift,
    gshift,
    slope1,
    slope2,
    prior_rs,
    prior_e,
    acc,
    sent,
    arrived,
    tiled,
    core_in,
    half,
    half_out,
    y_in,
    x_in,
    full,
    right_tiles,
    right_tmp,
    rc_in,
    r2,
    ry_in,
    load_sem,
    relay_send,
    relay_recv,
    core_send,
    core_recv,
    y_send,
    y_recv,
    x_send,
    x_recv,
    gy_send,
    gy_recv,
    gc_send,
    gc_recv,
    rc_send,
    rc_recv,
    ry_send,
    ry_recv,
):
    sections, nodes, locals_ = sizes
    across = nodes // 2
    replicas = nodes * locals_
    section = lax.axis_index("section")
    node = lax.axis_index("node")
    local = lax.axis_index("local")
    core = lax.rem(node, 2)
    column = lax.div(node, 2)
    buddy = node + 1 - 2 * core
    share = TILED // 2 // locals_
    half_rows = TILED // 2
    e_rows = OUT // replicas
    r_rows = MID // replicas
    below = (lax.rem(section + sections - 1, sections), node, local)
    above = (lax.rem(section + 1, sections), node, local)

    def y_peer(d):
        return (section, node, lax.rem(local + d, locals_))

    def x_peer(d):
        return (section, lax.rem(column + d, across) * 2 + core, local)

    def plane_peer(dx, dy):
        return (section, lax.rem(column + dx, across) * 2 + core, lax.rem(local + dy, locals_))

    other_core = (section, buddy, local)

    pairs = (
        (x_ref, x),
        (wr_ref, wr),
        (ws_ref, ws),
        (grad_ref, grad),
        (we_ref, we),
        (er_ref, er),
        (es_ref, es),
        (ee_ref, ee),
        (loss_ref, loss),
    )
    loads = [pltpu.make_async_copy(a, b, load_sem.at[i]) for i, (a, b) in enumerate(pairs)]
    for load in loads:
        load.start()
    barrier = pltpu.get_barrier_semaphore()
    pl.semaphore_signal(barrier, inc=1, device_id=above, device_id_type=MESH)
    pl.semaphore_signal(barrier, inc=1, device_id=other_core, device_id_type=MESH)
    for d in range(1, locals_):
        pl.semaphore_signal(barrier, inc=1, device_id=y_peer(d), device_id_type=MESH)
    for d in range(1, across):
        pl.semaphore_signal(barrier, inc=1, device_id=x_peer(d), device_id_type=MESH)
    for dx in range(1, across):
        for dy in range(1, locals_):
            pl.semaphore_signal(barrier, inc=1, device_id=plane_peer(dx, dy), device_id_type=MESH)

    def remote(src, dst, send, recv, device):
        return pltpu.make_async_remote_copy(
            src_ref=src, dst_ref=dst, send_sem=send, recv_sem=recv, device_id=device, device_id_type=MESH
        )

    spread[...] = spread_matrix()
    pad_rows = BLOCK - ROWS
    for t in range(TICKS):
        pad = pl.ds(t * BLOCK + ROWS, pad_rows)
        x_all[pad, :] = jnp.zeros((pad_rows, OUT), BF16)
        up_all[pad, :] = jnp.zeros((pad_rows, OUT), BF16)
        cols[pad, :] = jnp.zeros((pad_rows, TAPS), BF16)
        h2_all[pad, :] = jnp.zeros((pad_rows, MID), BF16)
        ga_all[pad, :] = jnp.zeros((pad_rows, MID), BF16)
        gb_all[pad, :] = jnp.zeros((pad_rows, MID), BF16)
    for b in range(3):
        for ref in (shift, gshift):
            ref[b, :PITCH, :] = jnp.zeros((PITCH, MID), BF16)
            ref[b, PITCH + ROWS :, :] = jnp.zeros((PITCH, MID), BF16)
    prior_rs[0] = two_terms(pr_ref[...])
    prior_rs[1] = two_terms(ps_ref[...])
    prior_e[...] = two_terms(pe_ref[...])

    def rows_of(t):
        return pl.ds(t * BLOCK, ROWS)

    def block_of(t):
        return pl.ds(t * BLOCK, BLOCK)

    def forward_one(t):
        x_all[rows_of(t), :] = dot(spread[...], x[:, t, :]).astype(BF16)
        pre1 = dot(x_all[rows_of(t), :], wr[...])
        q1 = sigmoid(pre1)
        pixel = lax.broadcasted_iota(jnp.int32, (ROWS, MID), 0) % PITCH < SIDE
        slope1[t % 2] = jnp.where(pixel, q1 * (1.0 + pre1 * (1.0 - q1)), 0.0)
        shifted_copies(pre1 * q1, shift)
        for a in range(3):
            for b in range(3):
                at = (3 * a + b) * MID
                cols[rows_of(t), at : at + MID] = shift[b, a * PITCH : a * PITCH + ROWS, :]

    def forward_two(t):
        pre2 = dot(cols[rows_of(t), :], ws[...])
        q2 = sigmoid(pre2)
        slope2[t % 2] = q2 * (1.0 + pre2 * (1.0 - q2))
        h2_all[rows_of(t), :] = (pre2 * q2).astype(BF16)

    def gb_rows(t, first, last):
        count = (last - first) * PITCH
        at = first * PITCH
        rows = pl.ds(t * BLOCK + at, count)
        if t > 0:
            is_last = jnp.full((count, OUT), section, jnp.int32) == sections - 1
            up_all[rows, :] = jnp.where(is_last, up_all[rows, :], arrived[t - 1, at : at + count, :])
        gb = (dot(up_all[rows, :], we_t[...]) * slope2[t % 2, at : at + count, :]).astype(BF16)
        gb_all[rows, :] = gb
        gb = gb.astype(F32)
        to = slice(PITCH + at, PITCH + at + count)
        gshift[1, to, :] = gb.astype(BF16)
        gshift[0, to, :] = pltpu.roll(gb, 1, 0).astype(BF16)
        gshift[2, to, :] = pltpu.roll(gb, count - 1, 0).astype(BF16)

    def ga_rows(t, first, last):
        count = (last - first) * PITCH
        at = first * PITCH
        for a in range(3):
            for b in range(3):
                tap = (3 * a + b) * MID
                gcols[at : at + count, tap : tap + MID] = gshift[
                    2 - b, (2 - a) * PITCH + at : (2 - a) * PITCH + at + count, :
                ]
        g1 = dot(gcols[at : at + count, :], ws_t[...])
        ga_all[pl.ds(t * BLOCK + at, count), :] = (g1 * slope1[t % 2, at : at + count, :]).astype(BF16)

    def dx_rows(t, first, last):
        rows = pl.ds(t * BLOCK + first * PITCH, (last - first) * PITCH)
        return (up_all[rows, :].astype(F32) + dot(ga_all[rows, :], wr_t[...])).astype(BF16)

    def left_late(t):
        a_r = two_terms(folded(dot_t(prior_rs[0], ga_all[block_of(t), :])))
        acc[:, :OUT] += dot(a_r, x_all[block_of(t), :])

    def left_early(t):
        a_s = two_terms(folded(dot_t(prior_rs[1], gb_all[block_of(t), :])))
        acc[:, OUT : OUT + TAPS] += dot(a_s, cols[block_of(t), :])
        a_e = two_terms(folded(dot_t(prior_e[...], up_all[block_of(t), :])))
        acc[:, OUT + TAPS :] += dot(a_e, h2_all[block_of(t), :])

    def fill(tiles):
        for j in tiles:
            at = placed(j) * RANK
            tiled[at : at + RANK, :] = (
                acc[:RANK, j * LANES : (j + 1) * LANES] + acc[RANK:, j * LANES : (j + 1) * LANES]
            )

    def piece(t, part):
        first = CUTS[part] - t if part else 0
        return first, CUTS[part + 1] - t if part < PIECES - 1 else SIDE

    relay = {}
    for t in range(TICKS - 1):
        for part in range(PIECES):
            first, last = piece(t, part)
            rows = pl.ds(first * PITCH, (last - first) * PITCH)
            sems = (relay_send.at[t, part], relay_recv.at[t, part])
            relay[t, part] = remote(sent.at[t, rows], arrived.at[t, rows], *sems, below)

    def arrive(count):
        for load in loads[arrive.done : count]:
            load.wait()
        arrive.done = count

    arrive.done = 0
    arrive(2)
    forward_one(0)
    arrive(3)
    forward_two(0)
    for k in range(9):
        ws_t[k * MID : (k + 1) * MID, :] = ws[k * MID : (k + 1) * MID, :].T
    arrive(5)
    we_t[...] = we[...].T
    wr_t[...] = wr[...].T
    up_all[rows_of(0), :] = dot(spread[...], grad[...]).astype(BF16)

    def shadow(t, part):
        if part == 0:
            arrive(5)
            forward_one(t + 1)
        elif part == 1:
            forward_two(t + 1)
        else:
            if t == 0:
                arrive(9)
                acc[:, :OUT] = dot_t(prior_rs[0], er[...])
                acc[:, OUT : OUT + TAPS] = dot_t(prior_rs[1], es[...])
                acc[:, OUT + TAPS :] = dot_t(prior_e[...], ee[...])
            up_all[rows_of(t + 1), :] = dot(spread[...], loss[t]).astype(BF16)
            left_late(t)
            left_early(t)

    mine = pl.ds(pl.multiple_of(core * half_rows, half_rows), half_rows)
    late = LATE_TILES * RANK
    to_core = []
    for i, (first, count) in enumerate(((late, half_rows - late), (0, late))):
        theirs = pl.ds(pl.multiple_of((1 - core) * half_rows + first, RANK), count)
        there = core_in.at[first : first + count]
        to_core.append(remote(tiled.at[theirs], there, core_send.at[i], core_recv.at[i], other_core))

    for t in range(TICKS):
        for part in range(PIECES):
            if t > 0:
                relay[t - 1, part].wait_recv()
                gb_rows(t, *piece(t - 1, part))
            elif part == 0:
                gb_rows(t, 0, SIDE)
            if t == TICKS - 1 and part == PIECES - 1:
                left_early(t)
                fill(range(OUT // LANES, COLUMNS // LANES))
                to_core[0].start()
            ga_rows(t, *piece(t, part))
            if t < TICKS - 1:
                first, last = piece(t, part)
                sent[t, first * PITCH : last * PITCH, :] = dx_rows(t, first, last)
                if t == 0 and part == 0:
                    pl.semaphore_wait(barrier, locals_ * across + 1)
                relay[t, part].start()
                shadow(t, part)
    left_late(TICKS - 1)
    fill(range(OUT // LANES))
    to_core[1].start()
    for copy in to_core:
        copy.wait_recv()
    half[...] = tiled[mine, :] + core_in[...]
    half_out[...] = half[...].astype(BF16)
    to_y = []
    for d in range(1, locals_):
        at = pl.multiple_of(lax.rem(local + d, locals_) * share, share)
        to_y.append(
            remote(half_out.at[pl.ds(at, share)], y_in.at[d - 1], y_send.at[d - 1], y_recv.at[d - 1], y_peer(d))
        )
        to_y[-1].start()
    leaving_ref[...] = dot(gather_matrix(), dx_rows(TICKS - 1, 0, SIDE)).astype(BF16)
    for copy in to_y:
        copy.wait_recv()
    summed = half[pl.ds(pl.multiple_of(local * share, share), share), :]
    for d in range(locals_ - 1):
        summed = summed + y_in[d].astype(F32)
    own = pl.ds(pl.multiple_of(core * half_rows + local * share, share), share)
    x_own = x_in.at[column]
    x_own[...] = summed
    to_x = []
    for d in range(1, across):
        to_x.append(remote(x_own, x_own, x_send.at[d - 1], x_recv.at[d - 1], x_peer(d)))
        to_x[-1].start()
    for copy in to_x:
        copy.wait_recv()
    summed = x_in[0]
    for d in range(1, across):
        summed = summed + x_in[d]
    full[own, :] = summed.astype(BF16)
    from_y = []
    for d in range(1, locals_):
        from_y.append(remote(full.at[own], full.at[own], gy_send.at[d - 1], gy_recv.at[d - 1], y_peer(d)))
        from_y[-1].start()
    for copy in from_y:
        copy.wait_recv()
    from_core = remote(full.at[mine], full.at[mine], gc_send, gc_recv, other_core)
    from_core.start()

    def half_products(which):
        tiles = []
        for i in range(HALF_TILES):
            at = pl.multiple_of(which * half_rows + i * RANK, RANK)
            tiles.append(full[pl.ds(at, RANK), :])
        results = []
        first = 0
        for (_, width), inputs, errors in zip(HALVES, (x_all, cols, h2_all), (er, es, ee)):
            terms = jnp.concatenate(tiles[first : first + width // LANES], axis=1)
            first += width // LANES
            span = pl.ds(pl.multiple_of(which * width, LANES), width)
            results += [dot_t(terms, inputs[:, span]), dot(terms, errors[span, :]), dot_t(terms, terms)]
        return results

    products = half_products(core)
    from_core.wait_recv()
    products = [a + b for a, b in zip(products, half_products(1 - core))]
    sum_r = folded(dot(two_terms(products[0]), ga_all[...])) + products[1]
    sum_s = folded(dot(two_terms(products[3]), gb_all[...])) + products[4]
    sum_e = folded(dot(two_terms(products[6]), up_all[...])) + products[7]
    right_tiles[...] = jnp.concatenate([sum_e, jnp.zeros((LANES - RANK, OUT), F32)], axis=0).T
    zero = jnp.zeros((RANK, MID), F32)
    right_tmp[...] = jnp.concatenate([zero, sum_r, sum_s, zero], axis=0).T
    for i in range(r_rows):
        right_tiles[pl.ds(i, replicas, stride=e_rows), :] += right_tmp[pl.ds(i, replicas, stride=r_rows), :]

    group = locals_ * e_rows

    def group_at(column_, core_):
        return pl.ds(pl.multiple_of((column_ * 2 + core_) * group, group), group)

    to_core2 = []
    for i in range(across):
        to_core2.append(
            remote(right_tiles.at[group_at(i, 1 - core)], rc_in.at[i], rc_send.at[i], rc_recv.at[i], other_core)
        )
        to_core2[-1].start()

    row_id = lax.broadcasted_iota(jnp.int32, (RANK, RANK), 0)
    col_id = lax.broadcasted_iota(jnp.int32, (RANK, RANK), 1)
    left = [products[2], products[5], products[8]]
    inverse = [jnp.where(row_id == col_id, 1.0, 0.0) for _ in PARTS]

    def eliminate(steps):
        for k in steps:
            for m in range(3):
                factor = left[m][:, k : k + 1] * (1.0 / left[m][k : k + 1, k : k + 1])
                factor = jnp.where(row_id[:, :1] > k, factor, 0.0)
                row_left, row_inverse = left[m][k : k + 1, :], inverse[m][k : k + 1, :]
                left[m] = left[m] - factor * row_left
                inverse[m] = inverse[m] - factor * row_inverse

    for copy in to_core2:
        copy.wait_recv()
    for i in range(across):
        r2[i] = right_tiles[group_at(i, core), :] + rc_in[i]
    to_plane = []
    for dx in range(across):
        for dy in range(locals_):
            if dx + dy > 0:
                at = pl.multiple_of(lax.rem(local + dy, locals_) * e_rows, e_rows)
                source = r2.at[lax.rem(column + dx, across), pl.ds(at, e_rows)]
                slot = dx * locals_ + dy - 1
                sems = (ry_send.at[slot], ry_recv.at[slot])
                to_plane.append(remote(source, ry_in.at[slot], *sems, plane_peer(dx, dy)))
                to_plane[-1].start()
    eliminate(range(RANK))
    for m in range(3):
        pivots = jnp.sum(jnp.where(row_id == col_id, left[m], 0.0), axis=1, keepdims=True)
        inverse[m] = inverse[m] * lax.rsqrt(pivots)

    replica = node * locals_ + local
    for m, ref in enumerate((basis_r_ref, basis_s_ref, basis_e_ref)):
        start, rows = PARTS[m]
        width = rows // replicas
        at = start + replica * width
        first = at // LANES
        tiles = 1 if LANES % width == 0 else width // LANES + 2
        pieces = []
        for i in range(tiles):
            j = jnp.minimum(first + i, COLUMNS // LANES - 1)
            pieces.append(full[pl.ds(pl.multiple_of(placed(j) * RANK, RANK), RANK), :].astype(F32))
        window = pieces[0] if tiles == 1 else jnp.concatenate(pieces, axis=1)
        span = tiles * LANES
        window = pltpu.roll(window, lax.rem(span - (at - first * LANES), span), 1)
        if m == 1:
            ref[...] = precise_dot(inverse[m], window)[:, :width] * math.sqrt(rows)
        else:
            ref[...] = precise_dot_t(window.T[:width, :], inverse[m]) * math.sqrt(rows)

    for copy in to_plane:
        copy.wait_recv()
    total = r2[column, pl.ds(pl.multiple_of(local * e_rows, e_rows), e_rows), :]
    for slot in range(across * locals_ - 1):
        total = total + ry_in[slot]
    right_e_ref[...] = precise_dot_t(total[:, :RANK], inverse[2]) / (replicas * math.sqrt(MID))
    few = total[:, RANK : 2 * RANK]
    right_r_ref[...] = precise_dot_t(few, inverse[0])[:r_rows, :] / (replicas * math.sqrt(OUT))
    few = total[:, 2 * RANK : 3 * RANK]
    right_s_ref[...] = precise_dot_t(few, inverse[1])[:r_rows, :] / (replicas * math.sqrt(TAPS))

    for copy in (*relay.values(), *to_core, *to_y, *to_x, *from_y, from_core, *to_core2, *to_plane):
        copy.wait_send()


def hand_over(*refs):
    for source, target in zip(refs[:7], refs[7:]):
        target[...] = source[...]


def on_device(
    sizes,
    section_inputs,
    grad_in,
    loss_grad,
    w_reduce,
    w_spatial,
    w_expand,
    err_reduce,
    err_spatial,
    err_expand,
    prior_reduce,
    prior_spatial,
    prior_expand,
):
    sections, nodes, locals_ = sizes
    across = nodes // 2
    replicas = nodes * locals_
    share = TILED // 2 // locals_
    e_rows = OUT // replicas
    r_rows = MID // replicas
    group = locals_ * e_rows
    vmem = pl.BlockSpec(memory_space=pltpu.VMEM)
    dma = pltpu.SemaphoreType.DMA
    more = max(across - 1, 1)
    hbm = pl.BlockSpec(memory_space=pltpu.HBM)
    scratch = [
        pltpu.VMEM((PIXELS, TICKS, OUT), BF16),
        pltpu.VMEM((PIXELS, OUT), BF16),
        pltpu.VMEM((TICKS - 1, PIXELS, OUT), BF16),
        pltpu.VMEM((OUT, MID), BF16),
        pltpu.VMEM((TAPS, MID), BF16),
        pltpu.VMEM((MID, OUT), BF16),
        pltpu.VMEM((OUT, MID), BF16),
        pltpu.VMEM((TAPS, MID), BF16),
        pltpu.VMEM((MID, OUT), BF16),
        pltpu.VMEM((ROWS, PIXELS), BF16),
        pltpu.VMEM((TICKS * BLOCK, OUT), BF16),
        pltpu.VMEM((TICKS * BLOCK, TAPS), BF16),
        pltpu.VMEM((TICKS * BLOCK, MID), BF16),
        pltpu.VMEM((TICKS * BLOCK, MID), BF16),
        pltpu.VMEM((TICKS * BLOCK, MID), BF16),
        pltpu.VMEM((TICKS * BLOCK, OUT), BF16),
        pltpu.VMEM((TAPS, MID), BF16),
        pltpu.VMEM((MID, OUT), BF16),
        pltpu.VMEM((OUT, MID), BF16),
        pltpu.VMEM((ROWS, TAPS), BF16),
        pltpu.VMEM((3, ROWS + 2 * PITCH, MID), BF16),
        pltpu.VMEM((3, ROWS + 2 * PITCH, MID), BF16),
        pltpu.VMEM((2, ROWS, MID), F32),
        pltpu.VMEM((2, ROWS, MID), F32),
        pltpu.VMEM((2, 2 * RANK, MID), BF16),
        pltpu.VMEM((2 * RANK, OUT), BF16),
        pltpu.VMEM((2 * RANK, COLUMNS), F32),
        pltpu.VMEM((TICKS - 1, ROWS, OUT), BF16),
        pltpu.VMEM((TICKS - 1, ROWS, OUT), BF16),
        pltpu.VMEM((TILED, LANES), F32),
        pltpu.VMEM((TILED // 2, LANES), F32),
        pltpu.VMEM((TILED // 2, LANES), F32),
        pltpu.VMEM((TILED // 2, LANES), BF16),
        pltpu.VMEM((locals_ - 1, share, LANES), BF16),
        pltpu.VMEM((across, share, LANES), F32),
        pltpu.VMEM((TILED, LANES), BF16),
        pltpu.VMEM((OUT, LANES), F32),
        pltpu.VMEM((MID, LANES), F32),
        pltpu.VMEM((across, group, LANES), F32),
        pltpu.VMEM((across, group, LANES), F32),
        pltpu.VMEM((across * locals_ - 1, e_rows, LANES), F32),
        dma((9,)),
        dma((TICKS - 1, PIECES)),
        dma((TICKS - 1, PIECES)),
        dma((2,)),
        dma((2,)),
        dma((locals_ - 1,)),
        dma((locals_ - 1,)),
        dma((more,)),
        dma((more,)),
        dma((locals_ - 1,)),
        dma((locals_ - 1,)),
        dma,
        dma,
        dma((across,)),
        dma((across,)),
        dma((across * locals_ - 1,)),
        dma((across * locals_ - 1,)),
    ]
    shapes = (
        jax.ShapeDtypeStruct((PIXELS, OUT), BF16),
        jax.ShapeDtypeStruct((OUT // replicas, RANK), F32),
        jax.ShapeDtypeStruct((RANK, TAPS // replicas), F32),
        jax.ShapeDtypeStruct((MID // replicas, RANK), F32),
        jax.ShapeDtypeStruct((r_rows, RANK), F32),
        jax.ShapeDtypeStruct((r_rows, RANK), F32),
        jax.ShapeDtypeStruct((e_rows, RANK), F32),
    )
    results = pl.pallas_call(
        functools.partial(kernel, sizes),
        out_shape=shapes,
        in_specs=[hbm] * 9 + [vmem] * 3,
        out_specs=(vmem,) * 7,
        scratch_shapes=scratch,
        compiler_params=pltpu.CompilerParams(
            collective_id=0, has_side_effects=True, vmem_limit_bytes=56 * 1024 * 1024
        ),
        cost_estimate=pl.CostEstimate(flops=5_000_000_000, bytes_accessed=6_000_000, transcendentals=500_000),
    )(
        section_inputs[0, 0].transpose(1, 0, 2),
        grad_in[0, 0],
        loss_grad[0],
        w_reduce[0],
        w_spatial[0],
        w_expand[0],
        err_reduce[0, 0],
        err_spatial[0, 0],
        err_expand[0, 0],
        prior_reduce[0],
        prior_spatial[0],
        prior_expand[0],
    )
    leaving, basis_r, basis_s, *others = pl.pallas_call(
        hand_over, out_shape=shapes, in_specs=[vmem] * 7, out_specs=(vmem,) * 7
    )(*results)
    return (leaving[None, None], basis_r.T[None], basis_s[None], *(other.T[None] for other in others))


def solution(mesh):
    sizes = (mesh.shape["section"], mesh.shape["node"], mesh.shape["local"])
    replicas = ("node", "local")
    return jax.shard_map(
        functools.partial(on_device, sizes),
        mesh=mesh,
        in_specs=(
            P("section", replicas),
            P("section", replicas),
            P(replicas),
            P("section"),
            P("section"),
            P("section"),
            P("section", replicas),
            P("section", replicas),
            P("section", replicas),
            P("section"),
            P("section"),
            P("section"),
        ),
        out_specs=(
            P("section", replicas),
            P("section", None, replicas),
            P("section", None, replicas),
            P("section", None, replicas),
            P("section", None, replicas),
            P("section", None, replicas),
            P("section", None, replicas),
        ),
        check_vma=False,
    )
```

```python
import functools
import math

import jax
import jax.numpy as jnp
from jax import lax
from jax.experimental import pallas as pl
from jax.experimental.pallas import tpu as pltpu
from jax.sharding import PartitionSpec as P

SIDE = 14
PITCH = 16
ROWS = SIDE * PITCH
BLOCK = 256
PIXELS = SIDE * SIDE
TICKS = 4
OUT = 512
MID = 256
RANK = 32
TAPS = 9 * MID
CUTS = (0, 6, 10)
PIECES = len(CUTS)
COLUMNS = OUT + TAPS + MID
LANES = 128
TILED = COLUMNS // LANES * RANK
MESH = pl.DeviceIdType.MESH
F32 = jnp.float32
BF16 = jnp.bfloat16
PARTS = ((0, OUT), (OUT, TAPS), (OUT + TAPS, MID))


HALF_TILES = COLUMNS // LANES // 2
HALVES = ((0, OUT // 2), (OUT, TAPS // 2), (OUT + TAPS, MID // 2))
LATE_TILES = OUT // 2 // LANES


def tile_place(tile):
    place = 0
    for start, width in HALVES:
        first, count = start // LANES, width // LANES
        for half in range(2):
            inside = (tile >= first + half * count) & (tile < first + (half + 1) * count)
            here = half * HALF_TILES + place + tile - first - half * count
            yield inside, here
        place += count


def placed(tile):
    if isinstance(tile, int):
        return next(here for inside, here in tile_place(tile) if inside)
    at = 0
    for inside, here in tile_place(tile):
        at = jnp.where(inside, here, at)
    return at


def dot(a, b):
    return jnp.dot(a, b, preferred_element_type=F32)


def dot_t(a, b):
    return lax.dot_general(a, b, (((1,), (1,)), ((), ())), preferred_element_type=F32)


def precise_dot_t(a, b):
    return lax.dot_general(
        a, b, (((1,), (1,)), ((), ())), preferred_element_type=F32, precision=lax.Precision.HIGHEST
    )


def precise_dot(a, b):
    return jnp.dot(a, b, preferred_element_type=F32, precision=lax.Precision.HIGHEST)


def two_terms(values):
    high = values.astype(BF16)
    low = (values - high.astype(F32)).astype(BF16)
    return jnp.concatenate([high, low], axis=0)


def folded(values):
    return values[:RANK] + values[RANK:]


def sigmoid(values):
    return 1.0 / (1.0 + jnp.exp(-values))


def spread_matrix():
    row = lax.broadcasted_iota(jnp.int32, (ROWS, PIXELS), 0)
    pixel = lax.broadcasted_iota(jnp.int32, (ROWS, PIXELS), 1)
    hit = ((row // PITCH) * SIDE + row % PITCH == pixel) & (row % PITCH < SIDE)
    return jnp.where(hit, 1.0, 0.0).astype(BF16)


def gather_matrix():
    row = lax.broadcasted_iota(jnp.int32, (PIXELS, ROWS), 1)
    pixel = lax.broadcasted_iota(jnp.int32, (PIXELS, ROWS), 0)
    hit = ((row // PITCH) * SIDE + row % PITCH == pixel) & (row % PITCH < SIDE)
    return jnp.where(hit, 1.0, 0.0).astype(BF16)


def shifted_copies(values, ref):
    ref[1, PITCH : PITCH + ROWS, :] = values.astype(BF16)
    ref[0, PITCH : PITCH + ROWS, :] = pltpu.roll(values, 1, 0).astype(BF16)
    ref[2, PITCH : PITCH + ROWS, :] = pltpu.roll(values, ROWS - 1, 0).astype(BF16)


def kernel(
    sizes,
    x_ref,
    grad_ref,
    loss_ref,
    wr_ref,
    ws_ref,
    we_ref,
    er_ref,
    es_ref,
    ee_ref,
    pr_ref,
    ps_ref,
    pe_ref,
    leaving_ref,
    basis_r_ref,
    basis_s_ref,
    basis_e_ref,
    right_r_ref,
    right_s_ref,
    right_e_ref,
    x,
    grad,
    loss,
    wr,
    ws,
    we,
    er,
    es,
    ee,
    spread,
    x_all,
    cols,
    h2_all,
    ga_all,
    gb_all,
    up_all,
    ws_t,
    wr_t,
    we_t,
    gcols,
    shift,
    gshift,
    slope1,
    slope2,
    prior_rs,
    prior_e,
    acc,
    sent,
    arrived,
    tiled,
    core_in,
    half,
    half_out,
    y_in,
    x_in,
    full,
    right_tiles,
    right_tmp,
    rc_in,
    r2,
    ry_in,
    load_sem,
    relay_send,
    relay_recv,
    core_send,
    core_recv,
    y_send,
    y_recv,
    x_send,
    x_recv,
    gy_send,
    gy_recv,
    gc_send,
    gc_recv,
    rc_send,
    rc_recv,
    ry_send,
    ry_recv,
):
    sections, nodes, locals_ = sizes
    across = nodes // 2
    replicas = nodes * locals_
    section = lax.axis_index("section")
    node = lax.axis_index("node")
    local = lax.axis_index("local")
    core = lax.rem(node, 2)
    column = lax.div(node, 2)
    buddy = node + 1 - 2 * core
    share = TILED // 2 // locals_
    half_rows = TILED // 2
    e_rows = OUT // replicas
    r_rows = MID // replicas
    below = (lax.rem(section + sections - 1, sections), node, local)
    above = (lax.rem(section + 1, sections), node, local)

    def y_peer(d):
        return (section, node, lax.rem(local + d, locals_))

    def x_peer(d):
        return (section, lax.rem(column + d, across) * 2 + core, local)

    def plane_peer(dx, dy):
        return (section, lax.rem(column + dx, across) * 2 + core, lax.rem(local + dy, locals_))

    other_core = (section, buddy, local)

    pairs = (
        (x_ref, x),
        (wr_ref, wr),
        (ws_ref, ws),
        (grad_ref, grad),
        (we_ref, we),
        (er_ref, er),
        (es_ref, es),
        (ee_ref, ee),
        (loss_ref, loss),
    )
    loads = [pltpu.make_async_copy(a, b, load_sem.at[i]) for i, (a, b) in enumerate(pairs)]
    for load in loads:
        load.start()
    barrier = pltpu.get_barrier_semaphore()
    pl.semaphore_signal(barrier, inc=1, device_id=above, device_id_type=MESH)
    pl.semaphore_signal(barrier, inc=1, device_id=other_core, device_id_type=MESH)
    for d in range(1, locals_):
        pl.semaphore_signal(barrier, inc=1, device_id=y_peer(d), device_id_type=MESH)
    for d in range(1, across):
        pl.semaphore_signal(barrier, inc=1, device_id=x_peer(d), device_id_type=MESH)
    for dx in range(1, across):
        for dy in range(1, locals_):
            pl.semaphore_signal(barrier, inc=1, device_id=plane_peer(dx, dy), device_id_type=MESH)

    def remote(src, dst, send, recv, device):
        return pltpu.make_async_remote_copy(
            src_ref=src, dst_ref=dst, send_sem=send, recv_sem=recv, device_id=device, device_id_type=MESH
        )

    spread[...] = spread_matrix()
    pad_rows = BLOCK - ROWS
    for t in range(TICKS):
        pad = pl.ds(t * BLOCK + ROWS, pad_rows)
        x_all[pad, :] = jnp.zeros((pad_rows, OUT), BF16)
        up_all[pad, :] = jnp.zeros((pad_rows, OUT), BF16)
        cols[pad, :] = jnp.zeros((pad_rows, TAPS), BF16)
        h2_all[pad, :] = jnp.zeros((pad_rows, MID), BF16)
        ga_all[pad, :] = jnp.zeros((pad_rows, MID), BF16)
        gb_all[pad, :] = jnp.zeros((pad_rows, MID), BF16)
    for b in range(3):
        for ref in (shift, gshift):
            ref[b, :PITCH, :] = jnp.zeros((PITCH, MID), BF16)
            ref[b, PITCH + ROWS :, :] = jnp.zeros((PITCH, MID), BF16)
    prior_rs[0] = two_terms(pr_ref[...])
    prior_rs[1] = two_terms(ps_ref[...])
    prior_e[...] = two_terms(pe_ref[...])

    def rows_of(t):
        return pl.ds(t * BLOCK, ROWS)

    def block_of(t):
        return pl.ds(t * BLOCK, BLOCK)

    def forward_one(t):
        x_all[rows_of(t), :] = dot(spread[...], x[:, t, :]).astype(BF16)
        pre1 = dot(x_all[rows_of(t), :], wr[...])
        q1 = sigmoid(pre1)
        pixel = lax.broadcasted_iota(jnp.int32, (ROWS, MID), 0) % PITCH < SIDE
        slope1[t % 2] = jnp.where(pixel, q1 * (1.0 + pre1 * (1.0 - q1)), 0.0)
        shifted_copies(pre1 * q1, shift)
        for a in range(3):
            for b in range(3):
                at = (3 * a + b) * MID
                cols[rows_of(t), at : at + MID] = shift[b, a * PITCH : a * PITCH + ROWS, :]

    def forward_two(t):
        pre2 = dot(cols[rows_of(t), :], ws[...])
        q2 = sigmoid(pre2)
        slope2[t % 2] = q2 * (1.0 + pre2 * (1.0 - q2))
        h2_all[rows_of(t), :] = (pre2 * q2).astype(BF16)

    def gb_rows(t, first, last):
        count = (last - first) * PITCH
        at = first * PITCH
        rows = pl.ds(t * BLOCK + at, count)
        if t > 0:
            is_last = jnp.full((count, OUT), section, jnp.int32) == sections - 1
            up_all[rows, :] = jnp.where(is_last, up_all[rows, :], arrived[t - 1, at : at + count, :])
        gb = (dot(up_all[rows, :], we_t[...]) * slope2[t % 2, at : at + count, :]).astype(BF16)
        gb_all[rows, :] = gb
        gb = gb.astype(F32)
        to = slice(PITCH + at, PITCH + at + count)
        gshift[1, to, :] = gb.astype(BF16)
        gshift[0, to, :] = pltpu.roll(gb, 1, 0).astype(BF16)
        gshift[2, to, :] = pltpu.roll(gb, count - 1, 0).astype(BF16)

    def ga_rows(t, first, last):
        count = (last - first) * PITCH
        at = first * PITCH
        for a in range(3):
            for b in range(3):
                tap = (3 * a + b) * MID
                gcols[at : at + count, tap : tap + MID] = gshift[
                    2 - b, (2 - a) * PITCH + at : (2 - a) * PITCH + at + count, :
                ]
        g1 = dot(gcols[at : at + count, :], ws_t[...])
        ga_all[pl.ds(t * BLOCK + at, count), :] = (g1 * slope1[t % 2, at : at + count, :]).astype(BF16)

    def dx_rows(t, first, last):
        rows = pl.ds(t * BLOCK + first * PITCH, (last - first) * PITCH)
        return (up_all[rows, :].astype(F32) + dot(ga_all[rows, :], wr_t[...])).astype(BF16)

    def left_late(t):
        a_r = two_terms(folded(dot_t(prior_rs[0], ga_all[block_of(t), :])))
        acc[:, :OUT] += dot(a_r, x_all[block_of(t), :])

    def left_early(t):
        a_s = two_terms(folded(dot_t(prior_rs[1], gb_all[block_of(t), :])))
        acc[:, OUT : OUT + TAPS] += dot(a_s, cols[block_of(t), :])
        a_e = two_terms(folded(dot_t(prior_e[...], up_all[block_of(t), :])))
        acc[:, OUT + TAPS :] += dot(a_e, h2_all[block_of(t), :])

    def fill(tiles):
        for j in tiles:
            at = placed(j) * RANK
            tiled[at : at + RANK, :] = (
                acc[:RANK, j * LANES : (j + 1) * LANES] + acc[RANK:, j * LANES : (j + 1) * LANES]
            )

    def piece(t, part):
        first = CUTS[part] - t if part else 0
        return first, CUTS[part + 1] - t if part < PIECES - 1 else SIDE

    relay = {}
    for t in range(TICKS - 1):
        for part in range(PIECES):
            first, last = piece(t, part)
            rows = pl.ds(first * PITCH, (last - first) * PITCH)
            sems = (relay_send.at[t, part], relay_recv.at[t, part])
            relay[t, part] = remote(sent.at[t, rows], arrived.at[t, rows], *sems, below)

    def arrive(count):
        for load in loads[arrive.done : count]:
            load.wait()
        arrive.done = count

    arrive.done = 0
    arrive(2)
    forward_one(0)
    arrive(3)
    forward_two(0)
    for k in range(9):
        ws_t[k * MID : (k + 1) * MID, :] = ws[k * MID : (k + 1) * MID, :].T
    arrive(5)
    we_t[...] = we[...].T
    wr_t[...] = wr[...].T
    up_all[rows_of(0), :] = dot(spread[...], grad[...]).astype(BF16)

    def shadow(t, part):
        if part == 0:
            arrive(5)
            forward_one(t + 1)
        elif part == 1:
            forward_two(t + 1)
        else:
            if t == 0:
                arrive(9)
                acc[:, :OUT] = dot_t(prior_rs[0], er[...])
                acc[:, OUT : OUT + TAPS] = dot_t(prior_rs[1], es[...])
                acc[:, OUT + TAPS :] = dot_t(prior_e[...], ee[...])
            up_all[rows_of(t + 1), :] = dot(spread[...], loss[t]).astype(BF16)
            left_late(t)
            left_early(t)

    mine = pl.ds(pl.multiple_of(core * half_rows, half_rows), half_rows)
    late = LATE_TILES * RANK
    to_core = []
    for i, (first, count) in enumerate(((late, half_rows - late), (0, late))):
        theirs = pl.ds(pl.multiple_of((1 - core) * half_rows + first, RANK), count)
        there = core_in.at[first : first + count]
        to_core.append(remote(tiled.at[theirs], there, core_send.at[i], core_recv.at[i], other_core))

    for t in range(TICKS):
        for part in range(PIECES):
            if t > 0:
                relay[t - 1, part].wait_recv()
                gb_rows(t, *piece(t - 1, part))
            elif part == 0:
                gb_rows(t, 0, SIDE)
            if t == TICKS - 1 and part == PIECES - 1:
                left_early(t)
                fill(range(OUT // LANES, COLUMNS // LANES))
                to_core[0].start()
            ga_rows(t, *piece(t, part))
            if t < TICKS - 1:
                first, last = piece(t, part)
                sent[t, first * PITCH : last * PITCH, :] = dx_rows(t, first, last)
                if t == 0 and part == 0:
                    pl.semaphore_wait(barrier, locals_ * across + 1)
                relay[t, part].start()
                shadow(t, part)
    left_late(TICKS - 1)
    fill(range(OUT // LANES))
    to_core[1].start()
    for copy in to_core:
        copy.wait_recv()
    half[...] = tiled[mine, :] + core_in[...]
    half_out[...] = half[...].astype(BF16)
    to_y = []
    for d in range(1, locals_):
        at = pl.multiple_of(lax.rem(local + d, locals_) * share, share)
        to_y.append(
            remote(half_out.at[pl.ds(at, share)], y_in.at[d - 1], y_send.at[d - 1], y_recv.at[d - 1], y_peer(d))
        )
        to_y[-1].start()
    leaving_ref[...] = dot(gather_matrix(), dx_rows(TICKS - 1, 0, SIDE)).astype(BF16)
    for copy in to_y:
        copy.wait_recv()
    summed = half[pl.ds(pl.multiple_of(local * share, share), share), :]
    for d in range(locals_ - 1):
        summed = summed + y_in[d].astype(F32)
    own = pl.ds(pl.multiple_of(core * half_rows + local * share, share), share)
    x_own = x_in.at[column]
    x_own[...] = summed
    to_x = []
    for d in range(1, across):
        to_x.append(remote(x_own, x_own, x_send.at[d - 1], x_recv.at[d - 1], x_peer(d)))
        to_x[-1].start()
    for copy in to_x:
        copy.wait_recv()
    summed = x_in[0]
    for d in range(1, across):
        summed = summed + x_in[d]
    full[own, :] = summed.astype(BF16)
    from_y = []
    for d in range(1, locals_):
        from_y.append(remote(full.at[own], full.at[own], gy_send.at[d - 1], gy_recv.at[d - 1], y_peer(d)))
        from_y[-1].start()
    for copy in from_y:
        copy.wait_recv()
    from_core = remote(full.at[mine], full.at[mine], gc_send, gc_recv, other_core)
    from_core.start()

    def half_products(which):
        tiles = []
        for i in range(HALF_TILES):
            at = pl.multiple_of(which * half_rows + i * RANK, RANK)
            tiles.append(full[pl.ds(at, RANK), :])
        results = []
        first = 0
        for (_, width), inputs, errors in zip(HALVES, (x_all, cols, h2_all), (er, es, ee)):
            terms = jnp.concatenate(tiles[first : first + width // LANES], axis=1)
            first += width // LANES
            span = pl.ds(pl.multiple_of(which * width, LANES), width)
            results += [dot_t(terms, inputs[:, span]), dot(terms, errors[span, :]), dot_t(terms, terms)]
        return results

    products = half_products(core)
    from_core.wait_recv()
    products = [a + b for a, b in zip(products, half_products(1 - core))]
    sum_r = folded(dot(two_terms(products[0]), ga_all[...])) + products[1]
    sum_s = folded(dot(two_terms(products[3]), gb_all[...])) + products[4]
    sum_e = folded(dot(two_terms(products[6]), up_all[...])) + products[7]
    right_tiles[...] = jnp.concatenate([sum_e, jnp.zeros((LANES - RANK, OUT), F32)], axis=0).T
    zero = jnp.zeros((RANK, MID), F32)
    right_tmp[...] = jnp.concatenate([zero, sum_r, sum_s, zero], axis=0).T
    for i in range(r_rows):
        right_tiles[pl.ds(i, replicas, stride=e_rows), :] += right_tmp[pl.ds(i, replicas, stride=r_rows), :]

    group = locals_ * e_rows

    def group_at(column_, core_):
        return pl.ds(pl.multiple_of((column_ * 2 + core_) * group, group), group)

    to_core2 = []
    for i in range(across):
        to_core2.append(
            remote(right_tiles.at[group_at(i, 1 - core)], rc_in.at[i], rc_send.at[i], rc_recv.at[i], other_core)
        )
        to_core2[-1].start()

    row_id = lax.broadcasted_iota(jnp.int32, (RANK, RANK), 0)
    col_id = lax.broadcasted_iota(jnp.int32, (RANK, RANK), 1)
    left = [products[2], products[5], products[8]]
    inverse = [jnp.where(row_id == col_id, 1.0, 0.0) for _ in PARTS]

    def eliminate(steps):
        for k in steps:
            for m in range(3):
                factor = left[m][:, k : k + 1] * (1.0 / left[m][k : k + 1, k : k + 1])
                factor = jnp.where(row_id[:, :1] > k, factor, 0.0)
                row_left, row_inverse = left[m][k : k + 1, :], inverse[m][k : k + 1, :]
                left[m] = left[m] - factor * row_left
                inverse[m] = inverse[m] - factor * row_inverse

    for copy in to_core2:
        copy.wait_recv()
    for i in range(across):
        r2[i] = right_tiles[group_at(i, core), :] + rc_in[i]
    to_plane = []
    for dx in range(across):
        for dy in range(locals_):
            if dx + dy > 0:
                at = pl.multiple_of(lax.rem(local + dy, locals_) * e_rows, e_rows)
                source = r2.at[lax.rem(column + dx, across), pl.ds(at, e_rows)]
                slot = dx * locals_ + dy - 1
                sems = (ry_send.at[slot], ry_recv.at[slot])
                to_plane.append(remote(source, ry_in.at[slot], *sems, plane_peer(dx, dy)))
                to_plane[-1].start()
    eliminate(range(RANK))
    for m in range(3):
        pivots = jnp.sum(jnp.where(row_id == col_id, left[m], 0.0), axis=1, keepdims=True)
        inverse[m] = inverse[m] * lax.rsqrt(pivots)

    replica = node * locals_ + local
    for m, ref in enumerate((basis_r_ref, basis_s_ref, basis_e_ref)):
        start, rows = PARTS[m]
        width = rows // replicas
        at = start + replica * width
        first = at // LANES
        tiles = 1 if LANES % width == 0 else width // LANES + 2
        pieces = []
        for i in range(tiles):
            j = jnp.minimum(first + i, COLUMNS // LANES - 1)
            pieces.append(full[pl.ds(pl.multiple_of(placed(j) * RANK, RANK), RANK), :].astype(F32))
        window = pieces[0] if tiles == 1 else jnp.concatenate(pieces, axis=1)
        span = tiles * LANES
        window = pltpu.roll(window, lax.rem(span - (at - first * LANES), span), 1)
        if m == 1:
            ref[...] = precise_dot(inverse[m], window)[:, :width] * math.sqrt(rows)
        else:
            ref[...] = precise_dot_t(window.T[:width, :], inverse[m]) * math.sqrt(rows)

    for copy in to_plane:
        copy.wait_recv()
    total = r2[column, pl.ds(pl.multiple_of(local * e_rows, e_rows), e_rows), :]
    for slot in range(across * locals_ - 1):
        total = total + ry_in[slot]
    right_e_ref[...] = precise_dot_t(total[:, :RANK], inverse[2]) / (replicas * math.sqrt(MID))
    few = total[:, RANK : 2 * RANK]
    right_r_ref[...] = precise_dot_t(few, inverse[0])[:r_rows, :] / (replicas * math.sqrt(OUT))
    few = total[:, 2 * RANK : 3 * RANK]
    right_s_ref[...] = precise_dot_t(few, inverse[1])[:r_rows, :] / (replicas * math.sqrt(TAPS))

    for copy in (*relay.values(), *to_core, *to_y, *to_x, *from_y, from_core, *to_core2, *to_plane):
        copy.wait_send()


def hand_over(*refs):
    copies = [pltpu.make_async_copy(refs[i], refs[7 + i], refs[14].at[i]) for i in range(7)]
    for copy in copies:
        copy.start()
    for copy in copies:
        copy.wait()


def on_device(
    sizes,
    section_inputs,
    grad_in,
    loss_grad,
    w_reduce,
    w_spatial,
    w_expand,
    err_reduce,
    err_spatial,
    err_expand,
    prior_reduce,
    prior_spatial,
    prior_expand,
):
    sections, nodes, locals_ = sizes
    across = nodes // 2
    replicas = nodes * locals_
    share = TILED // 2 // locals_
    e_rows = OUT // replicas
    r_rows = MID // replicas
    group = locals_ * e_rows
    vmem = pl.BlockSpec(memory_space=pltpu.VMEM)
    dma = pltpu.SemaphoreType.DMA
    more = max(across - 1, 1)
    hbm = pl.BlockSpec(memory_space=pltpu.HBM)
    scratch = [
        pltpu.VMEM((PIXELS, TICKS, OUT), BF16),
        pltpu.VMEM((PIXELS, OUT), BF16),
        pltpu.VMEM((TICKS - 1, PIXELS, OUT), BF16),
        pltpu.VMEM((OUT, MID), BF16),
        pltpu.VMEM((TAPS, MID), BF16),
        pltpu.VMEM((MID, OUT), BF16),
        pltpu.VMEM((OUT, MID), BF16),
        pltpu.VMEM((TAPS, MID), BF16),
        pltpu.VMEM((MID, OUT), BF16),
        pltpu.VMEM((ROWS, PIXELS), BF16),
        pltpu.VMEM((TICKS * BLOCK, OUT), BF16),
        pltpu.VMEM((TICKS * BLOCK, TAPS), BF16),
        pltpu.VMEM((TICKS * BLOCK, MID), BF16),
        pltpu.VMEM((TICKS * BLOCK, MID), BF16),
        pltpu.VMEM((TICKS * BLOCK, MID), BF16),
        pltpu.VMEM((TICKS * BLOCK, OUT), BF16),
        pltpu.VMEM((TAPS, MID), BF16),
        pltpu.VMEM((MID, OUT), BF16),
        pltpu.VMEM((OUT, MID), BF16),
        pltpu.VMEM((ROWS, TAPS), BF16),
        pltpu.VMEM((3, ROWS + 2 * PITCH, MID), BF16),
        pltpu.VMEM((3, ROWS + 2 * PITCH, MID), BF16),
        pltpu.VMEM((2, ROWS, MID), F32),
        pltpu.VMEM((2, ROWS, MID), F32),
        pltpu.VMEM((2, 2 * RANK, MID), BF16),
        pltpu.VMEM((2 * RANK, OUT), BF16),
        pltpu.VMEM((2 * RANK, COLUMNS), F32),
        pltpu.VMEM((TICKS - 1, ROWS, OUT), BF16),
        pltpu.VMEM((TICKS - 1, ROWS, OUT), BF16),
        pltpu.VMEM((TILED, LANES), F32),
        pltpu.VMEM((TILED // 2, LANES), F32),
        pltpu.VMEM((TILED // 2, LANES), F32),
        pltpu.VMEM((TILED // 2, LANES), BF16),
        pltpu.VMEM((locals_ - 1, share, LANES), BF16),
        pltpu.VMEM((across, share, LANES), F32),
        pltpu.VMEM((TILED, LANES), BF16),
        pltpu.VMEM((OUT, LANES), F32),
        pltpu.VMEM((MID, LANES), F32),
        pltpu.VMEM((across, group, LANES), F32),
        pltpu.VMEM((across, group, LANES), F32),
        pltpu.VMEM((across * locals_ - 1, e_rows, LANES), F32),
        dma((9,)),
        dma((TICKS - 1, PIECES)),
        dma((TICKS - 1, PIECES)),
        dma((2,)),
        dma((2,)),
        dma((locals_ - 1,)),
        dma((locals_ - 1,)),
        dma((more,)),
        dma((more,)),
        dma((locals_ - 1,)),
        dma((locals_ - 1,)),
        dma,
        dma,
        dma((across,)),
        dma((across,)),
        dma((across * locals_ - 1,)),
        dma((across * locals_ - 1,)),
    ]
    shapes = (
        jax.ShapeDtypeStruct((PIXELS, OUT), BF16),
        jax.ShapeDtypeStruct((OUT // replicas, RANK), F32),
        jax.ShapeDtypeStruct((RANK, TAPS // replicas), F32),
        jax.ShapeDtypeStruct((MID // replicas, RANK), F32),
        jax.ShapeDtypeStruct((r_rows, RANK), F32),
        jax.ShapeDtypeStruct((r_rows, RANK), F32),
        jax.ShapeDtypeStruct((e_rows, RANK), F32),
    )
    results = pl.pallas_call(
        functools.partial(kernel, sizes),
        out_shape=shapes,
        in_specs=[hbm] * 9 + [vmem] * 3,
        out_specs=(vmem,) * 7,
        scratch_shapes=scratch,
        compiler_params=pltpu.CompilerParams(
            collective_id=0, has_side_effects=True, vmem_limit_bytes=56 * 1024 * 1024
        ),
        cost_estimate=pl.CostEstimate(flops=5_000_000_000, bytes_accessed=6_000_000, transcendentals=500_000),
    )(
        section_inputs[0, 0].transpose(1, 0, 2),
        grad_in[0, 0],
        loss_grad[0],
        w_reduce[0],
        w_spatial[0],
        w_expand[0],
        err_reduce[0, 0],
        err_spatial[0, 0],
        err_expand[0, 0],
        prior_reduce[0],
        prior_spatial[0],
        prior_expand[0],
    )
    leaving, basis_r, basis_s, *others = pl.pallas_call(
        hand_over, out_shape=shapes, in_specs=[hbm] * 7, out_specs=(hbm,) * 7, scratch_shapes=[dma((7,))]
    )(*results)
    return (leaving[None, None], basis_r.T[None], basis_s[None], *(other.T[None] for other in others))


def solution(mesh):
    sizes = (mesh.shape["section"], mesh.shape["node"], mesh.shape["local"])
    replicas = ("node", "local")
    return jax.shard_map(
        functools.partial(on_device, sizes),
        mesh=mesh,
        in_specs=(
            P("section", replicas),
            P("section", replicas),
            P(replicas),
            P("section"),
            P("section"),
            P("section"),
            P("section", replicas),
            P("section", replicas),
            P("section", replicas),
            P("section"),
            P("section"),
            P("section"),
        ),
        out_specs=(
            P("section", replicas),
            P("section", None, replicas),
            P("section", None, replicas),
            P("section", None, replicas),
            P("section", None, replicas),
            P("section", None, replicas),
            P("section", None, replicas),
        ),
        check_vma=False,
    )
```
